128 devices in a mesh: pool: 4 (over z), group: 4 (over x), tensor: 8 (over y, core).
Axes of the slice: x: 4, y: 4, z: 4, core: 2. Of those that a mesh axis runs over, the one named last changes fastest.
Arguments:
- tokens: bfloat16 [4, 2048, 8192], P('group', 'pool'), may hold values from -6 to 6
- input_norm_gain: bfloat16 [8192], replicated, may hold values from 0.5 to 1.5
- query_projection: bfloat16 [8192, 8192], P(None, 'tensor'), may hold values from -0.0625 to 0.0625
- key_projection: bfloat16 [8192, 1024], P(None, 'tensor'), may hold values from -0.0625 to 0.0625
- value_projection: bfloat16 [8192, 1024], P(None, 'tensor'), may hold values from -0.0625 to 0.0625
- query_bias_vector: bfloat16 [8192], P('tensor'), may hold values from -8 to 8
- key_bias_vector: bfloat16 [1024], P('tensor'), may hold values from -8 to 8
- value_bias_vector: bfloat16 [1024], P('tensor'), may hold values from -3 to 3
- adapter_down_factors: bfloat16 [32, 3, 64, 8192], P(('pool', 'group'), None, None, 'tensor'), may hold values from -0.0625 to 0.0625
- adapter_up_query: bfloat16 [32, 64, 8192], P(('pool', 'group'), None, 'tensor'), may hold values from -0.19921875 to 0.19921875
- adapter_up_key: bfloat16 [32, 64, 1024], P(('pool', 'group'), None, 'tensor'), may hold values from -0.19921875 to 0.19921875
- adapter_up_value: bfloat16 [32, 64, 1024], P(('pool', 'group'), None, 'tensor'), may hold values from -0.19921875 to 0.19921875
- group_adapter_ids: int32 [4], replicated, may hold values from 0 to 31
- lengths: int32 [4, 3], P('group'), may hold values from 1 to 1024, 2048 in all within a row
- page_slot_table: int32 [512], replicated, may hold values from 0 to 511, as said below
Outputs:
- attn_out: bfloat16 [4, 2048, 8192], P('group', 'pool', 'tensor')
- kv_store: bfloat16 [512, 8, 2, 16, 128], P(('pool', 'group'), 'tensor')
The draws below stay inside these ranges and needn't reach their ends.
Inputs may be any that keep to these rules, and one draw needn't show every extreme that they name: `page_slot_table`: A permutation of the 512 storage slots; slot s lies on owner s // 32, where the device at pool index a and group index b is owner a * 4 + b. The 32 pages whose tokens one index of pool holds within one group map exactly 2 to each owner.
All inputs are finite; a program needn't handle non-finite values.
Results may differ from the reference program's by a relative error of at most 0.012.
Values may be sent and summed in bfloat16 or wider, within the bound.
A program may use at most 192 MiB of HBM per device.

```python
import math
import jax
import jax.numpy as jnp
import numpy as np
from jax import lax

MODEL_WIDTH = 8192
QUERY_HEADS = 64
KEY_VALUE_HEADS = 8
HEAD_SIZE = 128
ADAPTER_RANK = 64
PAGE_TOKENS = 16
REQS = 3
GROUP_TOKENS = 2048
GROUPS = 4
OWNERS = 16
BANK_SLOTS = 32
PAGES_DEV = 32
NPAGES = 512
PAGE_CAP = 2
MOSTLEN = 1024


def draw_key_bias_vector(key, part):
    key = jax.random.fold_in(key, 3)
    return jnp.clip(0.5 * jax.random.normal(key, (KEY_VALUE_HEADS * HEAD_SIZE,), jnp.float32), -3.0, 3.0).astype(jnp.bfloat16)


def draw_query_bias_vector(key, part):
    key = jax.random.fold_in(key, 5)
    return jnp.clip(0.5 * jax.random.normal(key, (QUERY_HEADS * HEAD_SIZE,), jnp.float32), -3.0, 3.0).astype(jnp.bfloat16)


def draw_page_slot_table(key, part):
    key = jax.random.fold_in(key, 7)
    source_keys = jax.random.split(jax.random.fold_in(key, 1), OWNERS)
    ordering = jax.vmap(lambda subkey: jax.random.permutation(subkey, PAGES_DEV))(source_keys)
    target = ordering % OWNERS
    arrival = ordering // OWNERS
    owner_keys = jax.random.split(jax.random.fold_in(key, 2), OWNERS)
    places = jax.vmap(lambda subkey: jax.random.permutation(subkey, PAGES_DEV))(owner_keys)
    source = jnp.arange(OWNERS, dtype=jnp.int32)[:, None]
    within = places[target, source * PAGE_CAP + arrival]
    slots = target * PAGES_DEV + within
    return slots.reshape(OWNERS // GROUPS, GROUPS, PAGES_DEV).transpose(1, 0, 2).reshape(NPAGES).astype(jnp.int32)


def with_ends(drawn, rng, low, largest):
    index_at = [jax.random.randint(jax.random.fold_in(rng, axis), (), 0, length) for axis, length in enumerate(drawn.shape)]
    longest = drawn.shape.index(max(drawn.shape))
    beside = index_at[:longest] + [(index_at[longest] + 1) % drawn.shape[longest]] + index_at[longest + 1:]
    return drawn.at[tuple(index_at)].set(low).at[tuple(beside)].set(largest)


def level_of(stream_key, dims, cuts, low, largest):
    def one(dim, shards_of):
        draws = jax.random.uniform(jax.random.fold_in(jax.random.fold_in(stream_key, 6), dim), (shards_of,), jnp.float32, low / len(cuts), largest / len(cuts))
        return jnp.repeat(jnp.exp(draws), dims[dim] // shards_of).reshape((-1,) + (1,) * (len(dims) - dim - 1))

    loudness = one(*cuts[0])
    for cut in cuts[1:]:
        loudness = loudness * one(*cut)
    return loudness


def profile(count, total, reach, slope):
    portions = [(1 << 20) // math.isqrt(grade ** slope) + 1 for grade in range(2, count + 1)]
    spare, counts = total - reach - (count - 1), [1] * (count - 1)
    while spare > 0:
        candidates = [i for i in range(count - 1) if counts[i] < reach]
        pool, left = sum([portions[i] for i in candidates]), spare
        for i in candidates:
            addition = min(reach - counts[i], max(1, left * portions[i] // pool), spare)
            counts[i] = counts[i] + addition
            spare = spare - addition
    return np.array([reach] + counts)


def uneven(own_key, amount, total, bound, slope):
    if amount == 2:
        one = jax.random.randint(own_key, (), max(1, total - bound), min(bound, total - 1) + 1)
        return jnp.stack([one, total - one])
    sizes = jnp.asarray(profile(amount, total, bound, slope), jnp.int32)
    pairs = (amount - 1) // 2
    giver, receiver = sizes[1:1 + 2 * pairs:2], sizes[2:2 + 2 * pairs:2]
    room = jnp.minimum(giver - 1, bound - receiver)
    passed = jax.random.randint(jax.random.fold_in(own_key, 1), (pairs,), 0, 1 << 20) % (room + 1)
    sizes = sizes.at[1:1 + 2 * pairs:2].set(giver - passed).at[2:2 + 2 * pairs:2].set(receiver + passed)
    return sizes[jax.random.permutation(jax.random.fold_in(own_key, 2), amount)]


def centred(stream_key, extent, spread, limit, pieces=(), kind=jnp.bfloat16):
    factor_of = level_of(stream_key, extent, pieces, -0.22, 0.18) if pieces else 1.0
    values = jax.random.normal(stream_key, extent, jnp.float32) * spread * factor_of
    return jnp.minimum(jnp.maximum(values, -limit), limit).astype(kind)


def setup_inputs(seed: int = 0) -> dict:
    key_of = jax.random.split(jax.random.key(seed), 16)
    return {
        "tokens": centred(key_of[0], (GROUPS, GROUP_TOKENS, MODEL_WIDTH), 1.0, 6.0, ((0, 4), (1, 4))),
        "input_norm_gain": jnp.clip(1.0 + 0.1 * jax.random.normal(key_of[1], (MODEL_WIDTH,), jnp.float32), 0.5, 1.5).astype(jnp.bfloat16),
        "query_projection": centred(key_of[2], (MODEL_WIDTH, QUERY_HEADS * HEAD_SIZE), MODEL_WIDTH ** -0.5, 0.0625, ((1, 8),)),
        "key_projection": centred(key_of[3], (MODEL_WIDTH, KEY_VALUE_HEADS * HEAD_SIZE), MODEL_WIDTH ** -0.5, 0.0625, ((1, 8),)),
        "value_projection": centred(key_of[4], (MODEL_WIDTH, KEY_VALUE_HEADS * HEAD_SIZE), MODEL_WIDTH ** -0.5, 0.0625, ((1, 8),)),
        "query_bias_vector": draw_query_bias_vector(jax.random.fold_in(key_of[15], 71), 0),
        "key_bias_vector": draw_key_bias_vector(jax.random.fold_in(key_of[15], 71), 0),
        "value_bias_vector": centred(key_of[7], (KEY_VALUE_HEADS * HEAD_SIZE,), 0.5, 3.0, ((0, 8),)),
        "adapter_down_factors": centred(key_of[8], (BANK_SLOTS, 3, ADAPTER_RANK, MODEL_WIDTH), MODEL_WIDTH ** -0.5, 0.0625, ((0, 16), (3, 8))),
        "adapter_up_query": centred(key_of[9], (BANK_SLOTS, ADAPTER_RANK, QUERY_HEADS * HEAD_SIZE), 0.03, 0.19921875, ((0, 16), (2, 8))),
        "adapter_up_key": centred(key_of[10], (BANK_SLOTS, ADAPTER_RANK, KEY_VALUE_HEADS * HEAD_SIZE), 0.03, 0.19921875, ((0, 16), (2, 8))),
        "adapter_up_value": centred(key_of[11], (BANK_SLOTS, ADAPTER_RANK, KEY_VALUE_HEADS * HEAD_SIZE), 0.03, 0.19921875, ((0, 16), (2, 8))),
        "group_adapter_ids": with_ends(jax.random.randint(key_of[12], (GROUPS,), 0, BANK_SLOTS), jax.random.fold_in(key_of[12], 1), 0, BANK_SLOTS - 1).astype(jnp.int32),
        "lengths": jax.vmap(lambda own: uneven(own, REQS, GROUP_TOKENS, MOSTLEN, 2))(jax.random.split(key_of[13], GROUPS)).reshape((GROUPS, REQS)).astype(jnp.int32),
        "page_slot_table": draw_page_slot_table(jax.random.fold_in(key_of[15], 71), 0),
    }


adapter_scale = 2.0
rope_theta = 1000000.0
norm_eps = 1e-06

def request_positions(lengths_row, token_count):
    request_end = jnp.cumsum(lengths_row).astype(jnp.int32)
    starts = (request_end - lengths_row).astype(jnp.int32)
    token_index = jnp.arange(token_count, dtype=jnp.int32)
    group_member = (token_index[:, None] >= starts[None, :]) & (token_index[:, None] < request_end[None, :])
    numbers = jnp.arange(lengths_row.shape[0], dtype=jnp.int32)
    segment = lax.optimization_barrier(jnp.sum(jnp.where(group_member, numbers[None, :], 0), axis=1)).astype(jnp.int32)
    page_offset = (token_index - lax.optimization_barrier(jnp.sum(jnp.where(group_member, starts[None, :], 0), axis=1))).astype(jnp.int32)
    return (segment, page_offset)

def apply_rotation(vectors, page_offset):
    half_dim = vectors.shape[-1] // 2
    frequency = rope_theta ** (-(jnp.arange(half_dim, dtype=jnp.float32) * 2.0 / vectors.shape[-1]))
    angle = page_offset.astype(jnp.float32)[:, None] * frequency[None, :]
    cosine = jnp.cos(angle)[:, None, :]
    sine_part = jnp.sin(angle)[:, None, :]
    first_half = vectors[..., :half_dim]
    second = vectors[..., half_dim:]
    return jnp.concatenate([first_half * cosine - second * sine_part, second * cosine + first_half * sine_part], axis=-1)

def rms_normalize(rows, input_norm_gain):
    widened = rows.astype(jnp.float32)
    row_scale = lax.rsqrt(lax.optimization_barrier(jnp.mean(widened * widened, axis=-1, keepdims=True)) + norm_eps)
    return (widened * row_scale * input_norm_gain.astype(jnp.float32)).astype(jnp.bfloat16)

def reference(tokens, input_norm_gain, query_projection, key_projection, value_projection, query_bias_vector, key_bias_vector, value_bias_vector, adapter_down_factors, adapter_up_query, adapter_up_key, adapter_up_value, group_adapter_ids, lengths, page_slot_table):
    query_per_key_ratio = QUERY_HEADS // KEY_VALUE_HEADS
    outputs = []
    page_list = []
    for group_index in range(GROUPS):
        adapter_slot_index = group_adapter_ids[group_index]
        down_factor_rows = lax.dynamic_index_in_dim(adapter_down_factors, adapter_slot_index, 0, keepdims=False)
        merged_weight = []
        for group_member, (frozen_weight, up_factor_bank) in enumerate(((query_projection, adapter_up_query), (key_projection, adapter_up_key), (value_projection, adapter_up_value))):
            up_factor = lax.dynamic_index_in_dim(up_factor_bank, adapter_slot_index, 0, keepdims=False)
            weight_update = jnp.dot(down_factor_rows[group_member].T, up_factor, preferred_element_type=jnp.float32)
            merged_weight.append((frozen_weight.astype(jnp.float32) + adapter_scale * weight_update).astype(jnp.bfloat16))
        normed = rms_normalize(tokens[group_index], input_norm_gain)
        query_rows = jnp.dot(normed, merged_weight[0], preferred_element_type=jnp.float32) + query_bias_vector.astype(jnp.float32)
        key_unrotated = jnp.dot(normed, merged_weight[1], preferred_element_type=jnp.float32) + key_bias_vector.astype(jnp.float32)
        value_projected = jnp.dot(normed, merged_weight[2], preferred_element_type=jnp.float32) + value_bias_vector.astype(jnp.float32)
        segment, page_offset = request_positions(lengths[group_index], GROUP_TOKENS)
        query_rows = (apply_rotation(query_rows.reshape(GROUP_TOKENS, QUERY_HEADS, HEAD_SIZE), page_offset) * HEAD_SIZE ** (-0.5)).astype(jnp.bfloat16)
        key_rotated = apply_rotation(key_unrotated.reshape(GROUP_TOKENS, KEY_VALUE_HEADS, HEAD_SIZE), page_offset).astype(jnp.bfloat16)
        value_row_block = value_projected.reshape(GROUP_TOKENS, KEY_VALUE_HEADS, HEAD_SIZE).astype(jnp.bfloat16)
        token_index = jnp.arange(GROUP_TOKENS, dtype=jnp.int32)
        allowed = (segment[:, None] == segment[None, :]) & (token_index[None, :] <= token_index[:, None])
        grouped_heads = query_rows.reshape(GROUP_TOKENS, KEY_VALUE_HEADS, query_per_key_ratio, HEAD_SIZE)

        def head_block_rows(kv_head):
            query_head = lax.dynamic_index_in_dim(grouped_heads, kv_head, 1, keepdims=False).astype(jnp.float32)
            key_head = lax.dynamic_index_in_dim(key_rotated, kv_head, 1, keepdims=False).astype(jnp.float32)
            value_head = lax.dynamic_index_in_dim(value_row_block, kv_head, 1, keepdims=False).astype(jnp.float32)
            scores = jnp.einsum('tgd,sd->gts', query_head, key_head)
            scores = jnp.where(allowed[None], scores, -jnp.inf)
            row_max = lax.optimization_barrier(jnp.max(scores, axis=-1, keepdims=True))
            weights = jnp.where(allowed[None], jnp.exp(scores - row_max), 0.0).astype(jnp.bfloat16)
            weights = lax.optimization_barrier(weights).astype(jnp.float32)
            row_sum = lax.optimization_barrier(jnp.sum(weights, axis=-1, keepdims=True))
            return jnp.einsum('gts,sd->gtd', weights, value_head) / row_sum
        head_rows = lax.map(head_block_rows, jnp.arange(KEY_VALUE_HEADS, dtype=jnp.int32))
        outputs.append(head_rows.transpose(2, 0, 1, 3).reshape(GROUP_TOKENS, QUERY_HEADS * HEAD_SIZE).astype(jnp.bfloat16))
        stacked_factors = jnp.stack([key_rotated, value_row_block], axis=1).reshape(GROUP_TOKENS // PAGE_TOKENS, PAGE_TOKENS, 2, KEY_VALUE_HEADS, HEAD_SIZE)
        page_list.append(stacked_factors.transpose(0, 3, 2, 1, 4))
    pages = jnp.concatenate(page_list, axis=0)
    stored = jnp.zeros_like(pages).at[page_slot_table].set(pages)
    return (jnp.stack(outputs, axis=0), stored)
```

```python
import functools
import math

import jax
import jax.numpy as jnp
import numpy as np
from jax import lax
from jax.experimental import pallas as pl
from jax.experimental.pallas import tpu as pltpu
from jax.sharding import PartitionSpec as P

HEAD = 128
PAGE = 16
RANK = 64
ADAPTER_SCALE = 2.0
ROPE_THETA = 1000000.0
EPS = 1e-06
MASKED = -1e30
BF = jnp.bfloat16
F32 = jnp.float32
MESH = pl.DeviceIdType.MESH
POOL = 4
GROUP = 4
OWNERS = 16
TENSOR = 8
TOK = 512
WIDTH = 8192
CHUNK = 1024
QCOLS = 1024
HEADS = 8
QB = 256
KWIN = 1280

IDS, LEN, SEND, RECV = 0, 4, 8, 40


def dot(a, b):
    return jnp.dot(a, b, preferred_element_type=F32)


def dot_t(a, b):
    return lax.dot_general(a, b, (((1,), (1,)), ((), ())), preferred_element_type=F32)


def kernel(
    tab, tokens, gain, wq, wk, wv, bias, down, upq, upk, upv, rope,
    out, store,
    x, wkv_b, wq_b, acc_kv, acc_q, sq, rsb, rope_b, cosb, sinb,
    r1kv, r1u, r1q, st_kv, st_u, st_q, dkv, upkv, dq, zst, zr, zs, zf,
    kvo, kvp, pst, prv, qbuf, qext, kext, kt,
    tok_sem, wkv_sem, wq_sem, rope_sem, loc_sem,
    s1kv, s1u, s1q, s2kv, s2u, s2q, srs, sag, skv, spg,
    r1kv_s, r1u_s, r1q_s, r2kv_s, r2u_s, r2q_s, rrs, rag, rkv, rpg,
):
    me_p = lax.axis_index("pool")
    me_g = lax.axis_index("group")
    me_t = lax.axis_index("tensor")
    owner = me_p * GROUP + me_g

    def tok_copy(c):
        return pltpu.make_async_copy(
            tokens.at[0, :, pl.ds(pl.multiple_of(c * CHUNK, CHUNK), CHUNK)], x.at[c], tok_sem.at[c]
        )

    def wkv_copy(c, which):
        src = (wk, wv)[which]
        return pltpu.make_async_copy(
            src.at[pl.ds(pl.multiple_of(c * CHUNK, CHUNK), CHUNK), :],
            wkv_b.at[c, :, pl.ds(which * HEAD, HEAD)],
            wkv_sem.at[c, which],
        )

    def wq_copy(j):
        return pltpu.make_async_copy(
            wq.at[:, pl.ds(j * 256, 256)], wq_b.at[j], wq_sem.at[j]
        )

    rope_copy = pltpu.make_async_copy(rope, rope_b, rope_sem)

    upkv[...] = jnp.zeros_like(upkv)
    dq[...] = jnp.zeros_like(dq)

    barrier = pltpu.get_barrier_semaphore()

    def plane(i):
        dest = lax.rem(owner + i, OWNERS)
        return dest // GROUP, lax.rem(dest, GROUP)

    @pl.loop(1, OWNERS)
    def _(i):
        dp, dg = plane(i)
        pl.semaphore_signal(barrier, inc=1, device_id=(dp, dg, me_t), device_id_type=MESH)

    @pl.loop(1, TENSOR)
    def _(i):
        dt = lax.rem(me_t + i, TENSOR)
        pl.semaphore_signal(barrier, inc=1, device_id=(me_p, me_g, dt), device_id_type=MESH)

    for c in range(2):
        tok_copy(c).start()
        wkv_copy(c, 0).start()
        wkv_copy(c, 1).start()

    pl.semaphore_wait(barrier, OWNERS - 1 + TENSOR - 1)

    def piece(i):
        dp, dg = plane(i)
        return dp, dg, pl.ds(pl.multiple_of(dp * 16, 16), 16), pl.ds(pl.multiple_of(dg * 256, 256), 256)

    mine2 = pl.ds(owner * 2, 2)
    my_rows = pl.ds(pl.multiple_of(me_p * 16, 16), 16)
    my_cols = pl.ds(pl.multiple_of(me_g * 256, 256), 256)

    def remote(src, dst, send, recv, dp, dg, dt):
        return pltpu.make_async_remote_copy(
            src_ref=src, dst_ref=dst, send_sem=send, recv_sem=recv,
            device_id=(dp, dg, dt), device_id_type=MESH,
        )

    def p1kv(i):
        dp, dg, rows, cols = piece(i)
        return remote(down.at[:, pl.ds(1, 2), rows, cols], r1kv.at[mine2], s1kv.at[i], r1kv_s.at[i], dp, dg, me_t)

    def p1q(i):
        dp, dg, rows, cols = piece(i)
        return (
            remote(down.at[:, 0, rows, cols], r1q.at[mine2, 0], s1q.at[0, i], r1q_s.at[0, i], dp, dg, me_t),
            remote(upq.at[:, rows, cols], r1q.at[mine2, 1], s1q.at[1, i], r1q_s.at[1, i], dp, dg, me_t),
        )

    def p1u(i):
        dp, dg, rows, _ = piece(i)
        return (
            remote(upk.at[:, rows, :], r1u.at[mine2, 0], s1u.at[0, i], r1u_s.at[0, i], dp, dg, me_t),
            remote(upv.at[:, rows, :], r1u.at[mine2, 1], s1u.at[1, i], r1u_s.at[1, i], dp, dg, me_t),
        )

    own1 = (
        pltpu.make_async_copy(down.at[:, pl.ds(1, 2), my_rows, my_cols], r1kv.at[mine2], loc_sem.at[0]),
        pltpu.make_async_copy(upk.at[:, my_rows, :], r1u.at[mine2, 0], loc_sem.at[1]),
        pltpu.make_async_copy(upv.at[:, my_rows, :], r1u.at[mine2, 1], loc_sem.at[2]),
        pltpu.make_async_copy(down.at[:, 0, my_rows, my_cols], r1q.at[mine2, 0], loc_sem.at[3]),
        pltpu.make_async_copy(upq.at[:, my_rows, my_cols], r1q.at[mine2, 1], loc_sem.at[4]),
    )

    @pl.loop(1, OWNERS)
    def _(i):
        p1kv(i).start()

    def to_column_zero(act):
        @pl.loop(0, POOL)
        def _(dp):
            i = lax.rem(dp * GROUP - owner + OWNERS, OWNERS)

            @pl.when(i != 0)
            def _():
                act(i)

    def from_column_zero(act):
        @pl.loop(0, POOL)
        def _(sp):
            i = lax.rem(owner - sp * GROUP + OWNERS, OWNERS)

            @pl.when(i != 0)
            def _():
                act(i)

    def start_both(pair):
        pair[0].start()
        pair[1].start()

    to_column_zero(lambda i: start_both(p1u(i)))
    for cp in own1:
        cp.start()

    @pl.loop(1, OWNERS)
    def _(i):
        start_both(p1q(i))

    for c in range(2, 8):
        tok_copy(c).start()
        wkv_copy(c, 0).start()
        wkv_copy(c, 1).start()
    rope_copy.start()
    for j in range(4):
        wq_copy(j).start()

    sq[...] = jnp.zeros_like(sq)
    acc_kv[...] = jnp.zeros_like(acc_kv)

    @pl.when(me_p < 1)
    def _():
        kvp[1] = jnp.zeros(kvp.shape[1:], BF)

    @pl.when(me_p < 2)
    def _():
        kvp[0] = jnp.zeros(kvp.shape[1:], BF)

    @pl.loop(0, 8)
    def _(c):
        tok_copy(c).wait()
        wkv_copy(c, 0).wait()
        wkv_copy(c, 1).wait()

        @pl.loop(0, TOK // 64)
        def _(r):
            rows = pl.ds(pl.multiple_of(r * 64, 64), 64)
            raw = x[c, rows, :].astype(F32)
            s = sq[rows, :]
            for k in range(CHUNK // 128):
                part = raw[:, k * 128 : (k + 1) * 128]
                s = s + part * part
            sq[rows, :] = s
            x[c, rows, :] = (raw * gain[c].astype(F32)).astype(BF)

        acc_kv[...] += dot(x[c], wkv_b[c])

    mean = jnp.sum(sq[...], axis=1, keepdims=True) * (1.0 / WIDTH)
    rsb[...] = jnp.broadcast_to(lax.rsqrt(mean + EPS), (TOK, HEAD))

    rope_copy.wait()
    start1 = tab[LEN]
    start2 = tab[LEN] + tab[LEN + 1]
    lane = lax.broadcasted_iota(jnp.int32, (TOK, HEAD), 1)
    low = lane < HEAD // 2
    token = me_p * TOK + lax.broadcasted_iota(jnp.int32, (TOK, HEAD), 0)

    def both(row, low_mask):
        turned = pltpu.roll(row, HEAD // 2, 1)
        return jnp.where(low_mask, row, turned), jnp.where(low_mask, turned, row)

    low8 = lax.broadcasted_iota(jnp.int32, (8, HEAD), 1) < HEAD // 2

    def start_row(at):
        return both(jnp.broadcast_to(rope_b[pl.ds(at, 1), :], (8, HEAD)), low8)

    c1, n1 = start_row(start1)
    c2, n2 = start_row(start2)
    tc, tn = both(rope_b[pl.ds(pl.multiple_of(me_p * TOK, TOK), TOK), :], low)
    in1 = token >= start1
    in2 = token >= start2
    sc = jnp.where(in2, c2[0:1, :], jnp.where(in1, c1[0:1, :], 1.0))
    sn = jnp.where(in2, n2[0:1, :], jnp.where(in1, n1[0:1, :], 0.0))
    cosb[...] = tc * sc + tn * sn
    turned = tn * sc - tc * sn
    sinb[...] = jnp.where(low, -turned, turned)

    segment = in1.astype(jnp.int32) + in2.astype(jnp.int32)
    qext[...] = jnp.where((lane < 4) & (lane != segment), MASKED, 0.0).astype(BF)
    row3 = lax.broadcasted_iota(jnp.int32, (HEAD, 3 * TOK), 0)
    ktok = (me_p - 2) * TOK + lax.broadcasted_iota(jnp.int32, (HEAD, 3 * TOK), 1)
    kseg = jnp.where(ktok < 0, 3, (ktok >= start1).astype(jnp.int32) + (ktok >= start2).astype(jnp.int32))
    kext[...] = (row3 == kseg).astype(F32).astype(BF)

    def p2kv(i):
        dp, dg = plane(i)
        return remote(st_kv.at[dg], dkv.at[:, my_rows, my_cols], s2kv.at[i], r2kv_s.at[i], dp, dg, me_t)

    def p2q(i):
        dp, dg = plane(i)
        return remote(st_q.at[dg], dq.at[:, my_rows, my_cols], s2q.at[i], r2q_s.at[i], dp, dg, me_t)

    up_low = pl.ds(pl.multiple_of(me_p * 16, 16), 16)
    up_high = pl.ds(pl.multiple_of(RANK + me_p * 16, 16), 16)

    def p2u(i):
        dp, dg = plane(i)
        return (
            remote(st_u.at[dg, 0], upkv.at[up_low, pl.ds(0, HEAD)], s2u.at[0, i], r2u_s.at[0, i], dp, dg, me_t),
            remote(st_u.at[dg, 1], upkv.at[up_high, pl.ds(HEAD, HEAD)], s2u.at[1, i], r2u_s.at[1, i], dp, dg, me_t),
        )

    own2 = (
        pltpu.make_async_copy(st_kv.at[me_g], dkv.at[:, my_rows, my_cols], loc_sem.at[5]),
        pltpu.make_async_copy(st_u.at[me_g, 0], upkv.at[up_low, pl.ds(0, HEAD)], loc_sem.at[6]),
        pltpu.make_async_copy(st_u.at[me_g, 1], upkv.at[up_high, pl.ds(HEAD, HEAD)], loc_sem.at[7]),
        pltpu.make_async_copy(st_q.at[me_g], dq.at[:, my_rows, my_cols], loc_sem.at[8]),
    )

    def wait_recv_both(pair):
        pair[0].wait_recv()
        pair[1].wait_recv()

    def second_kv():
        for k in range(3):
            own1[k].wait()

        @pl.loop(1, OWNERS)
        def _(i):
            p1kv(i).wait_recv()

        for g in range(GROUP):
            st_kv[g] = r1kv[tab[IDS + g]]

        @pl.loop(1, OWNERS)
        def _(i):
            p2kv(i).start()

        own2[0].start()

        @pl.when(me_g == 0)
        def _():
            @pl.loop(1, OWNERS)
            def _(i):
                wait_recv_both(p1u(i))

            for g in range(GROUP):
                st_u[g] = r1u[tab[IDS + g]]

            @pl.loop(1, OWNERS)
            def _(i):
                start_both(p2u(i))

            own2[1].start()
            own2[2].start()

    def second_q():
        own1[3].wait()
        own1[4].wait()

        @pl.loop(1, OWNERS)
        def _(i):
            wait_recv_both(p1q(i))

        for g in range(GROUP):
            st_q[g] = r1q[tab[IDS + g]]

        @pl.loop(1, OWNERS)
        def _(i):
            p2q(i).start()

        own2[3].start()

    def rs(w, i):
        dt = lax.rem(me_t + i, TENSOR)
        return remote(zst.at[w, dt], zr.at[w, i], srs.at[w, i], rrs.at[w, i], me_p, me_g, dt)

    def ag(w, i):
        dt = lax.rem(me_t + i, TENSOR)
        return remote(zs.at[w], zf.at[w, me_t], sag.at[w, i], rag.at[w, i], me_p, me_g, dt)

    def scatter(w, factors):
        z = dot_t(x[me_t], factors)
        zst[w] = z.astype(BF).reshape(TENSOR, TOK // TENSOR, HEAD)

        @pl.loop(1, TENSOR)
        def _(i):
            rs(w, i).start()

    def gather(w):
        total = zst[w, me_t].astype(F32)
        for i in range(1, TENSOR):
            rs(w, i).wait_recv()
            total = total + zr[w, i].astype(F32)
        summed = total.astype(BF)
        zs[w] = summed
        zf[w, me_t] = summed

        @pl.loop(1, TENSOR)
        def _(i):
            ag(w, i).start()

    def gathered(w):
        @pl.loop(1, TENSOR)
        def _(i):
            ag(w, i).wait_recv()

        return zf[w].reshape(TOK, HEAD)

    def q_tile(j):
        wq_copy(j).wait()
        cols = pl.ds(j * 256, 256)
        acc_q[:, cols] = dot(x[0], wq_b[j, pl.ds(0, CHUNK), :])

        @pl.loop(1, 8)
        def _(c):
            acc_q[:, cols] += dot(x[c], wq_b[j, pl.ds(pl.multiple_of(c * CHUNK, CHUNK), CHUNK), :])

    def rotated(v):
        return v * cosb[...] + pltpu.roll(v, HEAD // 2, 1) * sinb[...]

    second_kv()
    q_tile(0)

    @pl.loop(1, OWNERS)
    def _(i):
        p2kv(i).wait_recv()

    own2[0].wait()
    scatter(0, dkv[...].reshape(2 * RANK, CHUNK))
    second_q()
    q_tile(1)
    gather(0)

    @pl.loop(1, OWNERS)
    def _(i):
        p2q(i).wait_recv()

    own2[3].wait()
    scatter(1, dq[0])
    q_tile(2)

    from_column_zero(lambda i: wait_recv_both(p2u(i)))

    @pl.when(me_g == 0)
    def _():
        own2[1].wait()
        own2[2].wait()

    kv = acc_kv[...] + ADAPTER_SCALE * dot(gathered(0), upkv[...])
    key = rotated(kv[:, :HEAD] * rsb[...] + bias[:, pl.ds(QCOLS, HEAD)].astype(F32))
    value = kv[:, HEAD:] * rsb[...] + bias[:, pl.ds(QCOLS + HEAD, HEAD)].astype(F32)
    kvo[0] = key.astype(BF).reshape(TOK // PAGE, PAGE, HEAD)
    kvo[1] = value.astype(BF).reshape(TOK // PAGE, PAGE, HEAD)

    def ahead(step):
        return remote(kvo, kvp.at[2 - step], skv.at[step], rkv.at[step], me_p + step, me_g, me_t)

    @pl.when(me_p < POOL - 1)
    def _():
        ahead(1).start()

    @pl.when(me_p < POOL - 2)
    def _():
        ahead(2).start()

    def page_copy(i):
        dp, dg = plane(i)
        dest = dp * GROUP + dg
        return remote(pst.at[pl.ds(dest * 2, 2)], prv.at[mine2], spg.at[i], rpg.at[i], dp, dg, me_t)

    @pl.loop(0, 2 * OWNERS)
    def _(n):
        page = tab[SEND + n]
        pst[n, 0] = kvo[0, page]
        pst[n, 1] = kvo[1, page]

    @pl.loop(1, OWNERS)
    def _(i):
        page_copy(i).start()

    prv[mine2] = pst[mine2]

    gather(1)
    q_tile(3)

    zq = gathered(1)
    for j in range(4):
        cols = pl.ds(j * 256, 256)
        q = acc_q[:, cols] + ADAPTER_SCALE * dot(zq, dq[1, :, cols])
        for h in range(2):
            head = q[:, h * HEAD : (h + 1) * HEAD] * rsb[...] + bias[:, pl.ds(j * 256 + h * HEAD, HEAD)].astype(F32)
            qbuf[2 * j + h] = (rotated(head) * (HEAD**-0.5 * math.log2(math.e))).astype(BF)

    @pl.when(me_p >= 1)
    def _():
        ahead(1).wait_recv()

    @pl.when(me_p >= 2)
    def _():
        ahead(2).wait_recv()

    blocks = (kvp.at[0], kvp.at[1], kvo)
    for s in range(3):
        kt[:, pl.ds(s * TOK, TOK)] = blocks[s][0].reshape(TOK, HEAD).T

    ones = jnp.ones((KWIN, HEAD), BF)
    causal = lax.broadcasted_iota(jnp.int32, (QB, QB), 0) >= lax.broadcasted_iota(jnp.int32, (QB, QB), 1)

    for b in range(TOK // QB):
        rows = pl.ds(b * QB, QB)
        keys = jnp.concatenate([kt[:, pl.ds(b * QB, KWIN)], kext[:, pl.ds(b * QB, KWIN)]], axis=0)
        parts = [blocks[s][1].reshape(TOK, HEAD) for s in range(3)]
        values = jnp.concatenate(parts, axis=0)[b * QB : b * QB + KWIN]
        values = jnp.concatenate([values, ones], axis=1)

        @pl.loop(0, HEADS)
        def _(h):
            query = jnp.concatenate([qbuf[h, rows, :], qext[rows, :]], axis=1)
            score = dot(query, keys)
            last = jnp.where(causal, score[:, KWIN - QB :], MASKED)
            score = jnp.concatenate([score[:, : KWIN - QB], last], axis=1)
            top = jnp.max(score, axis=1, keepdims=True)
            weight = jnp.exp2(score - top).astype(BF)
            total = dot(weight, values)
            out[0, rows, pl.ds(pl.multiple_of(h * HEAD, HEAD), HEAD)] = (total[:, :HEAD] / total[:, HEAD:]).astype(BF)

    @pl.loop(1, OWNERS)
    def _(i):
        page_copy(i).wait_recv()

    @pl.loop(0, 2 * OWNERS)
    def _(n):
        store[n, 0] = prv[tab[RECV + n]]

    @pl.loop(1, OWNERS)
    def _(i):
        p1kv(i).wait_send()
        for cp in p1q(i):
            cp.wait_send()
        p2kv(i).wait_send()
        p2q(i).wait_send()
        page_copy(i).wait_send()

    def sent(pair):
        pair[0].wait_send()
        pair[1].wait_send()

    to_column_zero(lambda i: sent(p1u(i)))

    @pl.when(me_g == 0)
    def _():
        @pl.loop(1, OWNERS)
        def _(i):
            sent(p2u(i))

    @pl.loop(1, TENSOR)
    def _(i):
        for w in range(2):
            rs(w, i).wait_send()
            ag(w, i).wait_send()

    @pl.when(me_p < POOL - 1)
    def _():
        ahead(1).wait_send()

    @pl.when(me_p < POOL - 2)
    def _():
        ahead(2).wait_send()


def rope_table():
    positions = np.arange(2048, dtype=np.float64)[:, None]
    frequency = ROPE_THETA ** (-np.arange(64, dtype=np.float64) * 2.0 / HEAD)
    angle = positions * frequency[None, :]
    return np.concatenate([np.cos(angle), np.sin(angle)], axis=1).astype(np.float32)


def page_lists(table, me_p, me_g):
    owner = me_p * GROUP + me_g
    mine = lax.dynamic_slice_in_dim(table, me_g * 128 + me_p * 32, 32)
    number = jnp.arange(32, dtype=jnp.int32)
    order = jnp.sum((mine[None, :] < mine[:, None]).astype(jnp.int32), axis=1)
    send = jnp.sum(jnp.where(order[None, :] == number[:, None], number[None, :], 0), axis=1)
    slots = owner * 32 + number
    pages = jnp.arange(512, dtype=jnp.int32)
    sources = (pages % 128) // 32 * GROUP + pages // 128
    source = jnp.sum(jnp.where(table[None, :] == slots[:, None], sources[None, :], 0), axis=1)
    earlier = (source[None, :] == source[:, None]) & (number[None, :] < number[:, None])
    recv = source * 2 + jnp.sum(earlier.astype(jnp.int32), axis=1)
    return send, recv


def per_device(
    tokens, gain, wq, wk, wv, bq, bk, bv, down, upq, upk, upv, ids, lengths, table
):
    send, recv = page_lists(table, lax.axis_index("pool"), lax.axis_index("group"))
    tab = jnp.concatenate([ids, lengths[0], jnp.zeros((1,), jnp.int32), send, recv]).astype(jnp.int32)
    bias = jnp.concatenate([bq, bk, bv]).reshape(1, QCOLS + 2 * HEAD)
    smem = pl.BlockSpec(memory_space=pltpu.SMEM)
    vmem = pl.BlockSpec(memory_space=pltpu.VMEM)
    hbm = pl.BlockSpec(memory_space=pl.ANY)
    V = pltpu.VMEM
    D = pltpu.SemaphoreType.DMA
    scratch = [
        V((8, TOK, CHUNK), BF),
        V((8, CHUNK, 256), BF),
        V((4, WIDTH, 256), BF),
        V((TOK, 256), F32),
        V((TOK, QCOLS), F32),
        V((TOK, HEAD), F32),
        V((TOK, HEAD), F32),
        V((2048, HEAD), F32),
        V((TOK, HEAD), F32),
        V((TOK, HEAD), F32),
        V((32, 2, 16, 256), BF),
        V((32, 2, 16, HEAD), BF),
        V((32, 2, 16, 256), BF),
        V((4, 2, 16, 256), BF),
        V((4, 2, 16, HEAD), BF),
        V((4, 2, 16, 256), BF),
        V((2, RANK, CHUNK), BF),
        V((2 * RANK, 256), BF),
        V((2, 2 * RANK, CHUNK), BF),
        V((2, 8, 64, HEAD), BF),
        V((2, 8, 64, HEAD), BF),
        V((2, 64, HEAD), BF),
        V((2, 8, 64, HEAD), BF),
        V((2, 32, PAGE, HEAD), BF),
        V((2, 2, 32, PAGE, HEAD), BF),
        V((32, 2, PAGE, HEAD), BF),
        V((32, 2, PAGE, HEAD), BF),
        V((HEADS, TOK, HEAD), BF),
        V((TOK, HEAD), BF),
        V((HEAD, 3 * TOK), BF),
        V((HEAD, 3 * TOK), BF),
        D((8,)), D((8, 2)), D((4,)), D, D((9,)),
        D((16,)), D((2, 16)), D((2, 16)), D((16,)), D((2, 16)), D((16,)), D((2, 8)), D((2, 8)), D((3,)), D((16,)),
        D((16,)), D((2, 16)), D((2, 16)), D((16,)), D((2, 16)), D((16,)), D((2, 8)), D((2, 8)), D((3,)), D((16,)),
    ]
    return pl.pallas_call(
        kernel,
        out_shape=(
            jax.ShapeDtypeStruct((1, TOK, QCOLS), BF),
            jax.ShapeDtypeStruct((32, 1, 2, PAGE, HEAD), BF),
        ),
        in_specs=[smem, hbm, vmem, hbm, hbm, hbm, vmem, hbm, hbm, hbm, hbm, hbm],
        out_specs=(vmem, vmem),
        scratch_shapes=scratch,
        compiler_params=pltpu.CompilerParams(
            collective_id=0, has_side_effects=True, vmem_limit_bytes=60 * 1024 * 1024
        ),
        name="layer",
    )(tab, tokens, gain.reshape(8, 1, CHUNK), wq, wk, wv, bias, down, upq, upk, upv, jnp.asarray(rope_table()))


def solution(mesh):
    placed = (
        P("group", "pool", None),
        P(),
        P(None, "tensor"),
        P(None, "tensor"),
        P(None, "tensor"),
        P("tensor"),
        P("tensor"),
        P("tensor"),
        P(("pool", "group"), None, None, "tensor"),
        P(("pool", "group"), None, "tensor"),
        P(("pool", "group"), None, "tensor"),
        P(("pool", "group"), None, "tensor"),
        P(),
        P("group", None),
        P(),
    )
    return jax.shard_map(
        per_device,
        mesh=mesh,
        in_specs=placed,
        out_specs=(P("group", "pool", "tensor"), P(("pool", "group"), "tensor", None, None, None)),
        check_vma=False,
    )
```

```python
import functools
import math

import jax
import jax.numpy as jnp
import numpy as np
from jax import lax
from jax.experimental import pallas as pl
from jax.experimental.pallas import tpu as pltpu
from jax.sharding import PartitionSpec as P

HEAD = 128
PAGE = 16
RANK = 64
ADAPTER_SCALE = 2.0
ROPE_THETA = 1000000.0
EPS = 1e-06
MASKED = -1e30
BF = jnp.bfloat16
F32 = jnp.float32
MESH = pl.DeviceIdType.MESH
POOL = 4
GROUP = 4
OWNERS = 16
TENSOR = 8
TOK = 512
WIDTH = 8192
CHUNK = 1024
QCOLS = 1024
HEADS = 8
QB = 256
KWIN = 1280


def dot(a, b):
    return jnp.dot(a, b, preferred_element_type=F32)


def dot_t(a, b):
    return lax.dot_general(a, b, (((1,), (1,)), ((), ())), preferred_element_type=F32)


def kernel(
    ids, lengths, lists, tokens, vec, wq, wk, wv, down, upq, upk, upv, rope,
    out, store,
    x, wkv_b, wq_b, acc_kv, acc_q, sq, rsb, vecb, rope_b, cosb, sinb,
    r1, r1u, st, stu, fac, upkv, zst, zr, zs, zf,
    kvo, kvp, pst, prv, qx, kx, vx, top_b, sum_b,
    tok_sem, wkv_sem, wq_sem, misc, own_u,
    s1, s1u, s2, s2u, srs, sag, skv, spg,
    v1, v1u, v2, v2u, vrs, vag, vkv, vpg,
):
    me_p = lax.axis_index("pool")
    me_g = lax.axis_index("group")
    me_t = lax.axis_index("tensor")
    owner = me_p * GROUP + me_g

    def chunk(c):
        return pl.ds(pl.multiple_of(c * CHUNK, CHUNK), CHUNK)

    def tok_copy(c):
        return pltpu.make_async_copy(tokens.at[0, :, chunk(c)], x.at[c], tok_sem.at[c])

    def wkv_start(c):
        for n, src in enumerate((wk, wv)):
            pltpu.make_async_copy(src.at[chunk(c), :], wkv_b.at[c, :, pl.ds(n * HEAD, HEAD)], wkv_sem.at[c]).start()

    def arrived(ref, sem):
        pltpu.make_async_copy(ref, ref, sem).wait()

    def wq_copy(j):
        return pltpu.make_async_copy(wq.at[:, pl.ds(j * 256, 256)], wq_b.at[j], wq_sem.at[j])

    vec_copy = pltpu.make_async_copy(vec, vecb, misc.at[0])
    rope_copy = pltpu.make_async_copy(rope, rope_b, misc.at[1])

    upkv[...] = jnp.zeros_like(upkv)

    barrier = pltpu.get_barrier_semaphore()

    def plane(i):
        dest = lax.rem(owner + i, OWNERS)
        return dest // GROUP, lax.rem(dest, GROUP)

    def around(i):
        return lax.rem(me_t + i, TENSOR)

    @pl.loop(1, OWNERS)
    def _(i):
        dp, dg = plane(i)
        pl.semaphore_signal(barrier, inc=1, device_id=(dp, dg, me_t), device_id_type=MESH)

    @pl.loop(1, TENSOR)
    def _(i):
        pl.semaphore_signal(barrier, inc=1, device_id=(me_p, me_g, around(i)), device_id_type=MESH)

    vec_copy.start()
    for c in range(2):
        tok_copy(c).start()
        wkv_start(c)

    pl.semaphore_wait(barrier, OWNERS - 1 + TENSOR - 1)

    mine2 = pl.ds(owner * 2, 2)

    def rows_of(dp):
        return pl.ds(pl.multiple_of(dp * 16, 16), 16)

    def cols_of(dg):
        return pl.ds(pl.multiple_of(dg * 256, 256), 256)

    def remote(src, dst, send, recv, dp, dg, dt):
        return pltpu.make_async_remote_copy(
            src_ref=src, dst_ref=dst, send_sem=send, recv_sem=recv,
            device_id=(dp, dg, dt), device_id_type=MESH,
        )

    @pl.loop(1, OWNERS)
    def _(i):
        dp, dg = plane(i)
        rows, cols = rows_of(dp), cols_of(dg)
        remote(down.at[:, :, rows, cols], r1.at[mine2, pl.ds(0, 3)], s1, v1, dp, dg, me_t).start()
        remote(upq.at[:, rows, cols], r1.at[mine2, 3], s1, v1, dp, dg, me_t).start()

    pltpu.make_async_copy(down.at[:, :, rows_of(me_p), cols_of(me_g)], r1.at[mine2, pl.ds(0, 3)], v1).start()
    pltpu.make_async_copy(upq.at[:, rows_of(me_p), cols_of(me_g)], r1.at[mine2, 3], v1).start()

    for n, src in enumerate((upk, upv)):
        for dp in range(POOL):
            dest = dp * GROUP + n

            @pl.when(dest != owner)
            def _():
                remote(src.at[:, pl.ds(dp * 16, 16), :], r1u.at[mine2], s1u, v1u, dp, n, me_t).start()

        @pl.when(me_g == n)
        def _():
            pltpu.make_async_copy(src.at[:, rows_of(me_p), :], r1u.at[mine2], v1u).start()

    for c in range(2, 8):
        tok_copy(c).start()
        wkv_start(c)
    rope_copy.start()
    for j in range(4):
        wq_copy(j).start()

    sq[...] = jnp.zeros_like(sq)
    acc_kv[...] = jnp.zeros_like(acc_kv)
    vec_copy.wait()

    @pl.loop(0, 8)
    def _(c):
        tok_copy(c).wait()

        @pl.loop(0, TOK // 64)
        def _(r):
            rows = pl.ds(pl.multiple_of(r * 64, 64), 64)
            s = sq[rows, :]
            for k in range(CHUNK // 128):
                lanes = pl.ds(k * 128, 128)
                part = x[c, rows, lanes].astype(F32)
                s = s + part * part
                x[c, rows, lanes] = (part * vecb[pl.ds(c * 8 + k, 1), :]).astype(BF)
            sq[rows, :] = s

        arrived(wkv_b.at[c], wkv_sem.at[c])
        acc_kv[...] += dot(x[c], wkv_b[c])

    mean = jnp.sum(sq[...], axis=1, keepdims=True) * (1.0 / WIDTH)
    rsb[...] = jnp.broadcast_to(lax.rsqrt(mean + EPS), (TOK, HEAD))

    def q_tile(j):
        wq_copy(j).wait()
        cols = pl.ds(j * 256, 256)
        acc_q[:, cols] = dot(x[0], wq_b[j, pl.ds(0, CHUNK), :])

        @pl.loop(1, 8)
        def _(c):
            acc_q[:, cols] += dot(x[c], wq_b[j, chunk(c), :])

    q_tile(0)
    q_tile(1)
    q_tile(2)

    arrived(r1, v1)
    for g in range(GROUP):
        st[g] = r1[ids[g]]

    @pl.loop(1, OWNERS)
    def _(i):
        dp, dg = plane(i)
        remote(st.at[dg], fac.at[:, rows_of(me_p), cols_of(me_g)], s2, v2, dp, dg, me_t).start()

    pltpu.make_async_copy(st.at[me_g], fac.at[:, rows_of(me_p), cols_of(me_g)], v2).start()

    def up_place(n):
        first = RANK * (n + 1) + me_p * 16
        return upkv.at[pl.ds(pl.multiple_of(first, 16), 16), pl.ds(n * HEAD, HEAD)]

    for n in range(2):

        @pl.when(me_g == n)
        def _():
            arrived(r1u, v1u)
            for g in range(GROUP):
                stu[g] = r1u[ids[g]]

            @pl.loop(1, OWNERS)
            def _(i):
                dp, dg = plane(i)
                remote(stu.at[dg], up_place(n), s2u, v2u.at[n], dp, dg, me_t).start()

            pltpu.make_async_copy(stu.at[me_g], up_place(n), v2u.at[n]).start()

    rope_copy.wait()
    start1 = lengths[0, 0]
    start2 = lengths[0, 0] + lengths[0, 1]
    lane = lax.broadcasted_iota(jnp.int32, (TOK, HEAD), 1)
    low = lane < HEAD // 2
    token = me_p * TOK + lax.broadcasted_iota(jnp.int32, (TOK, HEAD), 0)

    def both(row, low_mask):
        turned = pltpu.roll(row, HEAD // 2, 1)
        return jnp.where(low_mask, row, turned), jnp.where(low_mask, turned, row)

    low8 = lax.broadcasted_iota(jnp.int32, (8, HEAD), 1) < HEAD // 2

    def start_row(at):
        return both(jnp.broadcast_to(rope_b[pl.ds(at, 1), :], (8, HEAD)), low8)

    c1, n1 = start_row(start1)
    c2, n2 = start_row(start2)
    tc, tn = both(rope_b[pl.ds(pl.multiple_of(me_p * TOK, TOK), TOK), :], low)
    in1 = token >= start1
    in2 = token >= start2
    sc = jnp.where(in2, c2[0:1, :], jnp.where(in1, c1[0:1, :], 1.0))
    sn = jnp.where(in2, n2[0:1, :], jnp.where(in1, n1[0:1, :], 0.0))
    cosb[...] = tc * sc + tn * sn
    swung = tn * sc - tc * sn
    sinb[...] = jnp.where(low, -swung, swung)

    segment = in1.astype(jnp.int32) + in2.astype(jnp.int32)
    marks = jnp.where((lane < 4) & (lane != segment), MASKED, 0.0).astype(BF)
    for h in range(HEADS):
        qx[h, :, pl.ds(HEAD, HEAD)] = marks
    mark_row = lax.broadcasted_iota(jnp.int32, (HEAD, 3 * TOK), 0)
    ktok = (me_p - 2) * TOK + lax.broadcasted_iota(jnp.int32, (HEAD, 3 * TOK), 1)
    kseg = (ktok >= start1).astype(jnp.int32) + (ktok >= start2).astype(jnp.int32)
    kx[pl.ds(HEAD, HEAD), :] = (mark_row == kseg).astype(F32).astype(BF)
    for n in range(3):
        vx[n, :, pl.ds(HEAD, HEAD)] = jnp.ones((TOK, HEAD), BF)

    arrived(fac, v2)
    z = dot_t(x[me_t], fac[...].reshape(4 * RANK, CHUNK))
    zst[...] = z.astype(BF).reshape(TENSOR, TOK // TENSOR, 4 * RANK)

    @pl.loop(1, TENSOR)
    def _(i):
        dt = around(i)
        remote(zst.at[dt], zr.at[i - 1], srs, vrs, me_p, me_g, dt).start()

    q_tile(3)
    arrived(zr, vrs)
    total = zst[me_t].astype(F32)
    for i in range(TENSOR - 1):
        total = total + zr[i].astype(F32)
    zs[...] = total.astype(BF)

    @pl.loop(1, TENSOR)
    def _(i):
        remote(zs, zf.at[me_t], sag, vag, me_p, me_g, around(i)).start()

    pltpu.make_async_copy(zs, zf.at[me_t], vag).start()
    for n in range(2):
        arrived(upkv.at[pl.ds(RANK * (n + 1), RANK), pl.ds(n * HEAD, HEAD)], v2u.at[n])
    arrived(zf, vag)
    low_rank = zf[...].reshape(TOK, 4 * RANK)

    def rotated(v):
        return v * cosb[...] + pltpu.roll(v, HEAD // 2, 1) * sinb[...]

    def bias(n):
        return vecb[pl.ds(64 + n, 1), :]

    kv = acc_kv[...] + ADAPTER_SCALE * dot(low_rank, upkv[...])
    key = rotated(kv[:, :HEAD] * rsb[...] + bias(8)).astype(BF)
    value = (kv[:, HEAD:] * rsb[...] + bias(9)).astype(BF)
    kvo[0] = key.reshape(TOK // PAGE, PAGE, HEAD)
    kvo[1] = value.reshape(TOK // PAGE, PAGE, HEAD)

    def ahead(step):
        return remote(kvo, kvp.at[2 - step], skv.at[step - 1], vkv.at[step - 1], me_p + step, me_g, me_t)

    for step in (1, 2):

        @pl.when(me_p < POOL - step)
        def _():
            ahead(step).start()

    @pl.loop(0, 2 * OWNERS)
    def _(n):
        page = lists[0, me_g * POOL + me_p, n]
        pst[n, 0] = kvo[0, page]
        pst[n, 1] = kvo[1, page]

    @pl.loop(1, OWNERS)
    def _(i):
        dp, dg = plane(i)
        dest = dp * GROUP + dg
        remote(pst.at[pl.ds(dest * 2, 2)], prv.at[mine2], spg, vpg, dp, dg, me_t).start()

    pltpu.make_async_copy(pst.at[mine2], prv.at[mine2], vpg).start()

    for j in range(4):
        q = acc_q[:, pl.ds(j * 256, 256)] + ADAPTER_SCALE * dot(low_rank[:, :RANK], fac[3, :, pl.ds(j * 256, 256)])
        for h in range(2):
            head = q[:, h * HEAD : (h + 1) * HEAD] * rsb[...] + bias(2 * j + h)
            qx[2 * j + h, :, pl.ds(0, HEAD)] = (rotated(head) * (HEAD**-0.5 * math.log2(math.e))).astype(BF)

    def place(n, ref):
        kx[pl.ds(0, HEAD), pl.ds(n * TOK, TOK)] = ref[0].reshape(TOK, HEAD).T
        vx[n, :, pl.ds(0, HEAD)] = ref[1].reshape(TOK, HEAD)

    causal = lax.broadcasted_iota(jnp.int32, (QB, QB), 0) >= lax.broadcasted_iota(jnp.int32, (QB, QB), 1)

    def attend(h, rows, n, first, count, diagonal):
        score = dot(qx[h, rows, :], kx[:, pl.ds(n * TOK + first, count)])
        if diagonal:
            last = jnp.where(causal, score[:, count - QB :], MASKED)
            score = last if count == QB else jnp.concatenate([score[:, : count - QB], last], axis=1)
        top = jnp.max(score, axis=1, keepdims=True)
        if not diagonal:
            before = top_b[h, rows, :]
            top = jnp.maximum(before[:, :1], top)
        weight = jnp.exp2(score - top).astype(BF)
        part = dot(weight, vx[n, pl.ds(first, count), :])
        wide = jnp.broadcast_to(top, (top.shape[0], HEAD))
        if not diagonal:
            fade = jnp.exp2(before - wide)
            part = part + sum_b[h, rows, :] * jnp.concatenate([fade, fade], axis=1)
        sum_b[h, rows, :] = part
        top_b[h, rows, :] = wide

    upper, lower, every = pl.ds(0, QB), pl.ds(QB, QB), pl.ds(0, TOK)
    place(2, kvo)

    @pl.loop(0, HEADS)
    def _(h):
        attend(h, upper, 2, 0, QB, True)
        attend(h, lower, 2, 0, TOK, True)

    @pl.when(me_p >= 1)
    def _():
        ahead(1).wait_recv()
        place(1, kvp.at[1])

        @pl.loop(0, HEADS)
        def _(h):
            attend(h, every, 1, 0, TOK, False)

    @pl.when(me_p >= 2)
    def _():
        ahead(2).wait_recv()
        place(0, kvp.at[0])

        @pl.loop(0, HEADS)
        def _(h):
            attend(h, upper, 0, 0, TOK, False)
            attend(h, lower, 0, QB, QB, False)

    @pl.loop(0, HEADS)
    def _(h):
        both_parts = sum_b[h]
        out[0, :, pl.ds(pl.multiple_of(h * HEAD, HEAD), HEAD)] = (both_parts[:, :HEAD] / both_parts[:, HEAD:]).astype(BF)

    arrived(prv, vpg)

    @pl.loop(0, 2 * OWNERS)
    def _(n):
        store[n, 0] = prv[lists[1, owner, n]]

    arrived(r1.at[pl.ds(0, 2 * (OWNERS - 1))], s1)
    arrived(r1.at[pl.ds(0, OWNERS - 1)], s2)
    arrived(zr, srs)
    arrived(zr, sag)
    arrived(prv.at[pl.ds(0, 2 * (OWNERS - 1))], spg)

    @pl.when(me_g < 2)
    def _():
        arrived(r1u.at[pl.ds(0, 2 * 7)], s1u)
        arrived(r1u.at[pl.ds(0, OWNERS - 1)], s2u)

    @pl.when(me_g >= 2)
    def _():
        arrived(r1u.at[pl.ds(0, 2 * 8)], s1u)

    for step in (1, 2):

        @pl.when(me_p < POOL - step)
        def _():
            ahead(step).wait_send()


def rope_table():
    positions = np.arange(2048, dtype=np.float64)[:, None]
    frequency = ROPE_THETA ** (-np.arange(64, dtype=np.float64) * 2.0 / HEAD)
    angle = positions * frequency[None, :]
    return np.concatenate([np.cos(angle), np.sin(angle)], axis=1).astype(np.float32)


def page_lists(table):
    slots = table.reshape(16, 32)
    number = jnp.arange(32, dtype=jnp.int32)
    order = jnp.sum((slots[:, None, :] < slots[:, :, None]).astype(jnp.int32), axis=2)
    send = jnp.sum(jnp.where(order[:, None, :] == number[None, :, None], number[None, None, :], 0), axis=2)
    pages = jnp.arange(512, dtype=jnp.int32)
    sources = (pages % 128) // 32 * GROUP + pages // 128
    wanted = pages.reshape(16, 32)
    source = jnp.sum(jnp.where(table[None, None, :] == wanted[:, :, None], sources[None, None, :], 0), axis=2)
    earlier = (source[:, None, :] == source[:, :, None]) & (number[None, None, :] < number[None, :, None])
    recv = source * 2 + jnp.sum(earlier.astype(jnp.int32), axis=2)
    return jnp.stack([send, recv])


def per_device(
    tokens, gain, wq, wk, wv, bq, bk, bv, down, upq, upk, upv, ids, lengths, table
):
    vec = jnp.concatenate([gain, bq, bk, bv]).astype(F32).reshape(74, HEAD)
    smem = pl.BlockSpec(memory_space=pltpu.SMEM)
    vmem = pl.BlockSpec(memory_space=pltpu.VMEM)
    hbm = pl.BlockSpec(memory_space=pl.ANY)
    V = pltpu.VMEM
    D = pltpu.SemaphoreType.DMA
    scratch = [
        V((8, TOK, CHUNK), BF),
        V((8, CHUNK, 256), BF),
        V((4, WIDTH, 256), BF),
        V((TOK, 256), F32),
        V((TOK, QCOLS), F32),
        V((TOK, HEAD), F32),
        V((TOK, HEAD), F32),
        V((74, HEAD), F32),
        V((2048, HEAD), F32),
        V((TOK, HEAD), F32),
        V((TOK, HEAD), F32),
        V((32, 4, 16, 256), BF),
        V((32, 16, HEAD), BF),
        V((4, 4, 16, 256), BF),
        V((4, 16, HEAD), BF),
        V((4, RANK, CHUNK), BF),
        V((4 * RANK, 256), BF),
        V((8, 64, 256), BF),
        V((7, 64, 256), BF),
        V((64, 256), BF),
        V((8, 64, 256), BF),
        V((2, 32, PAGE, HEAD), BF),
        V((2, 2, 32, PAGE, HEAD), BF),
        V((32, 2, PAGE, HEAD), BF),
        V((32, 2, PAGE, HEAD), BF),
        V((HEADS, TOK, 2 * HEAD), BF),
        V((2 * HEAD, 3 * TOK), BF),
        V((3, TOK, 2 * HEAD), BF),
        V((HEADS, TOK, HEAD), F32),
        V((HEADS, TOK, 2 * HEAD), F32),
        D((8,)), D((8,)), D((4,)), D((2,)), D,
        D, D, D, D, D, D, D((2,)), D,
        D, D, D, D((2,)), D, D, D((2,)), D,
    ]
    return pl.pallas_call(
        kernel,
        out_shape=(
            jax.ShapeDtypeStruct((1, TOK, QCOLS), BF),
            jax.ShapeDtypeStruct((32, 1, 2, PAGE, HEAD), BF),
        ),
        in_specs=[smem, smem, smem] + [hbm] * 10,
        out_specs=(vmem, vmem),
        scratch_shapes=scratch,
        compiler_params=pltpu.CompilerParams(
            collective_id=0, has_side_effects=True, vmem_limit_bytes=60 * 1024 * 1024
        ),
        name="layer",
    )(ids, lengths, page_lists(table), tokens, vec, wq, wk, wv, down, upq, upk, upv, jnp.asarray(rope_table()))


def solution(mesh):
    placed = (
        P("group", "pool", None),
        P(),
        P(None, "tensor"),
        P(None, "tensor"),
        P(None, "tensor"),
        P("tensor"),
        P("tensor"),
        P("tensor"),
        P(("pool", "group"), None, None, "tensor"),
        P(("pool", "group"), None, "tensor"),
        P(("pool", "group"), None, "tensor"),
        P(("pool", "group"), None, "tensor"),
        P(),
        P("group", None),
        P(),
    )
    return jax.shard_map(
        per_device,
        mesh=mesh,
        in_specs=placed,
        out_specs=(P("group", "pool", "tensor"), P(("pool", "group"), "tensor", None, None, None)),
        check_vma=False,
    )
```

```python
import functools
import math

import jax
import jax.numpy as jnp
import numpy as np
from jax import lax
from jax.experimental import pallas as pl
from jax.experimental.pallas import tpu as pltpu
from jax.sharding import PartitionSpec as P

HEAD = 128
PAGE = 16
RANK = 64
ADAPTER_SCALE = 2.0
ROPE_THETA = 1000000.0
EPS = 1e-06
MASKED = -1e30
BF = jnp.bfloat16
F32 = jnp.float32
MESH = pl.DeviceIdType.MESH
POOL = 4
GROUP = 4
OWNERS = 16
TENSOR = 8
TOK = 512
WIDTH = 8192
CHUNK = 1024
QCOLS = 1024
HEADS = 8
QB = 256
KWIN = 1280


def dot(a, b):
    return jnp.dot(a, b, preferred_element_type=F32)


def dot_t(a, b):
    return lax.dot_general(a, b, (((1,), (1,)), ((), ())), preferred_element_type=F32)


def kernel(
    ids, lengths, tokens, gain, wq, wk, wv, bq, bk, bv, down, upq, upk, upv, table, rope,
    out, store,
    x, wkv_b, wq_b, acc_kv, acc_q, sq, rsb, gain_b, bq_b, bk_b, bv_b, table_b, vecb, list_v, list_s, rope_b, cosb, sinb,
    r1, r1u, st, stu, fac, upkv, zst, zr, zs, zf, zp,
    kvo, kvb, kvp, pst, prv, qx, kx, vx, top_b, sum_b,
    tok_sem, wkv_sem, wq_sem, misc,
    s1, s1u, s2, s2u, srs, sag, skv, szp, spg,
    v1, v1u, v2, v2u, vrs, vag, vkv, vzp, vpg,
):
    me_p = lax.axis_index("pool")
    me_g = lax.axis_index("group")
    me_t = lax.axis_index("tensor")
    owner = me_p * GROUP + me_g

    def chunk(c):
        return pl.ds(pl.multiple_of(c * CHUNK, CHUNK), CHUNK)

    def tok_copy(c):
        return pltpu.make_async_copy(tokens.at[0, :, chunk(c)], x.at[c], tok_sem.at[c])

    def wkv_start(c):
        for n, src in enumerate((wk, wv)):
            pltpu.make_async_copy(src.at[chunk(c), :], wkv_b.at[c, :, pl.ds(n * HEAD, HEAD)], wkv_sem.at[c]).start()

    def arrived(ref, sem):
        pltpu.make_async_copy(ref, ref, sem).wait()

    def wq_copy(j):
        return pltpu.make_async_copy(wq.at[:, pl.ds(j * 256, 256)], wq_b.at[j], wq_sem.at[j])

    small = [
        pltpu.make_async_copy(src, dst, misc.at[2 + n])
        for n, (src, dst) in enumerate(((gain, gain_b), (bq, bq_b), (bk, bk_b), (bv, bv_b), (table, table_b)))
    ]
    rope_copy = pltpu.make_async_copy(rope, rope_b, misc.at[1])

    upkv[...] = jnp.zeros_like(upkv)

    barrier = pltpu.get_barrier_semaphore()

    def plane(i):
        dest = lax.rem(owner + i, OWNERS)
        return dest // GROUP, lax.rem(dest, GROUP)

    def around(i):
        return lax.rem(me_t + i, TENSOR)

    @pl.loop(1, OWNERS)
    def _(i):
        dp, dg = plane(i)
        pl.semaphore_signal(barrier, inc=1, device_id=(dp, dg, me_t), device_id_type=MESH)

    @pl.loop(1, TENSOR)
    def _(i):
        pl.semaphore_signal(barrier, inc=1, device_id=(me_p, me_g, around(i)), device_id_type=MESH)

    for cp in small:
        cp.start()
    for c in range(2):
        tok_copy(c).start()
        wkv_start(c)

    pl.semaphore_wait(barrier, OWNERS - 1 + TENSOR - 1)

    mine2 = pl.ds(owner * 2, 2)

    def rows_of(dp):
        return pl.ds(pl.multiple_of(dp * 16, 16), 16)

    def cols_of(dg):
        return pl.ds(pl.multiple_of(dg * 256, 256), 256)

    def remote(src, dst, send, recv, dp, dg, dt):
        return pltpu.make_async_remote_copy(
            src_ref=src, dst_ref=dst, send_sem=send, recv_sem=recv,
            device_id=(dp, dg, dt), device_id_type=MESH,
        )

    for n, src in enumerate((upk, upv)):
        for dp in range(POOL):
            dest = dp * GROUP + n

            @pl.when(dest != owner)
            def _():
                remote(src.at[:, pl.ds(dp * 16, 16), :], r1u.at[mine2], s1u, v1u, dp, n, me_t).start()

        @pl.when(me_g == n)
        def _():
            pltpu.make_async_copy(src.at[:, rows_of(me_p), :], r1u.at[mine2], v1u).start()

    @pl.loop(1, OWNERS)
    def _(i):
        dp, dg = plane(i)
        rows, cols = rows_of(dp), cols_of(dg)
        remote(down.at[:, :, rows, cols], r1.at[mine2, pl.ds(0, 3)], s1, v1, dp, dg, me_t).start()
        remote(upq.at[:, rows, cols], r1.at[mine2, 3], s1, v1, dp, dg, me_t).start()

    pltpu.make_async_copy(down.at[:, :, rows_of(me_p), cols_of(me_g)], r1.at[mine2, pl.ds(0, 3)], v1).start()
    pltpu.make_async_copy(upq.at[:, rows_of(me_p), cols_of(me_g)], r1.at[mine2, 3], v1).start()

    for c in range(2, 8):
        tok_copy(c).start()
        wkv_start(c)
    rope_copy.start()
    for j in range(4):
        wq_copy(j).start()

    sq[...] = jnp.zeros_like(sq)
    acc_kv[...] = jnp.zeros_like(acc_kv)
    for cp in small:
        cp.wait()
    for c in range(8):
        vecb[pl.ds(c * 8, 8), :] = gain_b[pl.ds(c * CHUNK, CHUNK)].astype(F32).reshape(8, HEAD)
    vecb[pl.ds(64, 8), :] = bq_b[...].astype(F32).reshape(8, HEAD)
    vecb[pl.ds(72, 1), :] = bk_b[...].astype(F32).reshape(1, HEAD)
    vecb[pl.ds(73, 1), :] = bv_b[...].astype(F32).reshape(1, HEAD)

    @pl.loop(0, 8)
    def _(c):
        tok_copy(c).wait()

        @pl.loop(0, TOK // 64)
        def _(r):
            rows = pl.ds(pl.multiple_of(r * 64, 64), 64)
            s = sq[rows, :]
            for k in range(CHUNK // 128):
                lanes = pl.ds(k * 128, 128)
                part = x[c, rows, lanes].astype(F32)
                s = s + part * part
                x[c, rows, lanes] = (part * vecb[pl.ds(c * 8 + k, 1), :]).astype(BF)
            sq[rows, :] = s

        arrived(wkv_b.at[c], wkv_sem.at[c])
        acc_kv[...] += dot(x[c], wkv_b[c])

    mean = jnp.sum(sq[...], axis=1, keepdims=True) * (1.0 / WIDTH)
    rsb[...] = jnp.broadcast_to(lax.rsqrt(mean + EPS), (TOK, HEAD))

    def bias(n):
        return vecb[pl.ds(64 + n, 1), :]

    def q_tile(j):
        wq_copy(j).wait()
        cols = pl.ds(j * 256, 256)
        acc_q[:, cols] = dot(x[0], wq_b[j, pl.ds(0, CHUNK), :])

        @pl.loop(1, 8)
        def _(c):
            acc_q[:, cols] += dot(x[c], wq_b[j, chunk(c), :])

    kv_base = acc_kv[...] * jnp.concatenate([rsb[...], rsb[...]], axis=1)
    kv_base = kv_base + jnp.concatenate([bias(8), bias(9)], axis=1)
    acc_kv[...] = kv_base
    kvb[...] = kv_base.astype(BF)

    def make_lists():
        shape = (32, HEAD)
        list_v[...] = jnp.zeros_like(list_v)
        sub = lax.broadcasted_iota(jnp.int32, shape, 0)
        lan = lax.broadcasted_iota(jnp.int32, shape, 1)
        slots = table_b[...].reshape(4, HEAD)
        wide = [jnp.broadcast_to(slots[r : r + 1, :], shape) for r in range(4)]
        mine = jnp.where(me_g < 2, jnp.where(me_g == 0, wide[0], wide[1]), jnp.where(me_g == 2, wide[2], wide[3]))
        first = me_p * 32

        def column(v, where):
            return jnp.sum(jnp.where(where, v, 0), axis=1, keepdims=True)

        def row(v, where):
            return jnp.sum(jnp.where(where, v, 0), axis=0, keepdims=True)

        own = column(mine, lan == sub + first)
        inside = (lan >= first) & (lan < first + 32)
        order = column(1, inside & (mine < own))
        list_v[pl.ds(0, 1), :] = row(sub, order == lan)
        source = jnp.zeros((32, 1), jnp.int32)
        for r in range(4):
            source = source + column(lan // 32 * GROUP + r, wide[r] == sub + owner * 32)
        as_row = row(jnp.broadcast_to(source, shape), lan == sub)
        item = source * 2 + column(1, (as_row == source) & (lan < sub))
        list_v[pl.ds(1, 1), :] = row(jnp.broadcast_to(item, shape), lan == sub)
        pltpu.make_async_copy(list_v, list_s, misc.at[0]).start()

    q_tile(0)
    q_tile(1)

    arrived(r1, v1)
    for g in range(GROUP):
        st[g, pl.ds(0, 2)] = r1[ids[g], pl.ds(1, 2)]
        st[g, 2] = r1[ids[g], 0]
        st[g, 3] = r1[ids[g], 3]

    @pl.loop(1, OWNERS)
    def _(i):
        dp, dg = plane(i)
        remote(st.at[dg], fac.at[:, rows_of(me_p), cols_of(me_g)], s2, v2, dp, dg, me_t).start()

    pltpu.make_async_copy(st.at[me_g], fac.at[:, rows_of(me_p), cols_of(me_g)], v2).start()

    def up_place(n):
        first = RANK * n + me_p * 16
        return upkv.at[pl.ds(pl.multiple_of(first, 16), 16), pl.ds(n * HEAD, HEAD)]

    for n in range(2):

        @pl.when(me_g == n)
        def _():
            arrived(r1u, v1u)
            for g in range(GROUP):
                stu[g] = r1u[ids[g]]

            @pl.loop(1, OWNERS)
            def _(i):
                dp, dg = plane(i)
                remote(stu.at[dg], up_place(n), s2u, v2u.at[n], dp, dg, me_t).start()

            pltpu.make_async_copy(stu.at[me_g], up_place(n), v2u.at[n]).start()

    q_tile(2)
    make_lists()

    arrived(fac, v2)

    def ahead(step):
        return remote(kvb, kvp.at[2 - step], skv.at[step - 1], vkv.at[step - 1], me_p + step, me_g, me_t)

    def ahead_z(step):
        return remote(
            zf.at[:, :, pl.ds(0, HEAD)], zp.at[2 - step], szp.at[step - 1], vzp.at[step - 1], me_p + step, me_g, me_t
        )

    for step in (1, 2):

        @pl.when(me_p < POOL - step)
        def _():
            ahead(step).start()

    z = dot_t(x[me_t], fac[...].reshape(4 * RANK, CHUNK))
    zst[...] = z.astype(BF).reshape(TENSOR, TOK // TENSOR, 4 * RANK)

    @pl.loop(1, TENSOR)
    def _(i):
        dt = around(i)
        remote(zst.at[dt], zr.at[i - 1], srs, vrs, me_p, me_g, dt).start()

    q_tile(3)
    arrived(zr, vrs)
    total = zst[me_t].astype(F32)
    for i in range(TENSOR - 1):
        total = total + zr[i].astype(F32)
    mine = rsb[pl.ds(pl.multiple_of(me_t * 64, 64), 64), :] * ADAPTER_SCALE
    zs[...] = (total * jnp.concatenate([mine, mine], axis=1)).astype(BF)

    @pl.loop(1, TENSOR)
    def _(i):
        remote(zs, zf.at[me_t], sag, vag, me_p, me_g, around(i)).start()

    pltpu.make_async_copy(zs, zf.at[me_t], vag).start()
    rope_copy.wait()
    start1 = lengths[0, 0]
    start2 = lengths[0, 0] + lengths[0, 1]
    lane = lax.broadcasted_iota(jnp.int32, (TOK, HEAD), 1)
    low = lane < HEAD // 2

    def both(row, low_mask):
        turned = pltpu.roll(row, HEAD // 2, 1)
        return jnp.where(low_mask, row, turned), jnp.where(low_mask, turned, row)

    low8 = lax.broadcasted_iota(jnp.int32, (8, HEAD), 1) < HEAD // 2

    def start_row(at):
        return both(jnp.broadcast_to(rope_b[pl.ds(at, 1), :], (8, HEAD)), low8)

    c1, n1 = start_row(start1)
    c2, n2 = start_row(start2)

    def rotation(n):
        first = (me_p + (n - 2)) * TOK
        token = first + lax.broadcasted_iota(jnp.int32, (TOK, HEAD), 0)
        tc, tn = both(rope_b[pl.ds(pl.multiple_of(first, TOK), TOK), :], low)
        in1 = token >= start1
        in2 = token >= start2
        sc = jnp.where(in2, c2[0:1, :], jnp.where(in1, c1[0:1, :], 1.0))
        sn = jnp.where(in2, n2[0:1, :], jnp.where(in1, n1[0:1, :], 0.0))
        cosb[n] = tc * sc + tn * sn
        swung = tn * sc - tc * sn
        sinb[n] = jnp.where(low, -swung, swung)
        return in1.astype(jnp.int32) + in2.astype(jnp.int32)

    segment = rotation(2)
    marks = jnp.where((lane < 4) & (lane != segment), MASKED, 0.0).astype(BF)
    for h in range(HEADS):
        qx[h, :, pl.ds(HEAD, HEAD)] = marks
    mark_row = lax.broadcasted_iota(jnp.int32, (HEAD, 3 * TOK), 0)
    ktok = (me_p - 2) * TOK + lax.broadcasted_iota(jnp.int32, (HEAD, 3 * TOK), 1)
    kseg = (ktok >= start1).astype(jnp.int32) + (ktok >= start2).astype(jnp.int32)
    kx[pl.ds(HEAD, HEAD), :] = (mark_row == kseg).astype(F32).astype(BF)
    for n in range(3):
        vx[n, :, pl.ds(HEAD, HEAD)] = jnp.ones((TOK, HEAD), BF)
    for n in range(2):

        @pl.when(me_p + n >= 2)
        def _():
            rotation(n)

    for n in range(2):
        arrived(upkv.at[pl.ds(RANK * n, RANK), pl.ds(n * HEAD, HEAD)], v2u.at[n])
    arrived(zf, vag)
    for step in (1, 2):

        @pl.when(me_p < POOL - step)
        def _():
            ahead_z(step).start()

    def rotated(v, n):
        return v * cosb[n] + pltpu.roll(v, HEAD // 2, 1) * sinb[n]

    def finish(n, base, z):
        kv = base + dot(z, upkv[...])
        key = rotated(kv[:, :HEAD], n).astype(BF)
        value = kv[:, HEAD:].astype(BF)
        kx[pl.ds(0, HEAD), pl.ds(n * TOK, TOK)] = key.T
        vx[n, :, pl.ds(0, HEAD)] = value
        return key, value

    key, value = finish(2, acc_kv[...], zf[:, :, pl.ds(0, HEAD)].reshape(TOK, HEAD))
    kvo[0] = key.reshape(TOK // PAGE, PAGE, HEAD)
    kvo[1] = value.reshape(TOK // PAGE, PAGE, HEAD)

    pltpu.make_async_copy(list_v, list_s, misc.at[0]).wait()

    @pl.loop(0, 2 * OWNERS)
    def _(n):
        page = jnp.clip(list_s[0, n], 0, 31)
        pst[n, 0] = kvo[0, page]
        pst[n, 1] = kvo[1, page]

    @pl.loop(1, OWNERS)
    def _(i):
        dp, dg = plane(i)
        dest = dp * GROUP + dg
        remote(pst.at[pl.ds(dest * 2, 2)], prv.at[mine2], spg, vpg, dp, dg, me_t).start()

    pltpu.make_async_copy(pst.at[mine2], prv.at[mine2], vpg).start()

    for j in range(4):
        low_rank = dot(zf[:, :, pl.ds(HEAD, HEAD)].reshape(TOK, HEAD)[:, :RANK], fac[3, :, pl.ds(j * 256, 256)])
        for h in range(2):
            head = acc_q[:, pl.ds(j * 256 + h * HEAD, HEAD)] * rsb[...] + bias(2 * j + h)
            head = head + low_rank[:, h * HEAD : (h + 1) * HEAD]
            qx[2 * j + h, :, pl.ds(0, HEAD)] = (rotated(head, 2) * (HEAD**-0.5 * math.log2(math.e))).astype(BF)

    causal = lax.broadcasted_iota(jnp.int32, (QB, QB), 0) >= lax.broadcasted_iota(jnp.int32, (QB, QB), 1)

    def attend(h, rows, n, first, count, diagonal):
        score = dot(qx[h, rows, :], kx[:, pl.ds(n * TOK + first, count)])
        if diagonal:
            last = jnp.where(causal, score[:, count - QB :], MASKED)
            score = last if count == QB else jnp.concatenate([score[:, : count - QB], last], axis=1)
        top = jnp.max(score, axis=1, keepdims=True)
        if not diagonal:
            before = top_b[h, rows, :]
            top = jnp.maximum(before[:, :1], top)
        weight = jnp.exp2(score - top).astype(BF)
        part = dot(weight, vx[n, pl.ds(first, count), :])
        wide = jnp.broadcast_to(top, (top.shape[0], HEAD))
        if not diagonal:
            fade = jnp.exp2(before - wide)
            part = part + sum_b[h, rows, :] * jnp.concatenate([fade, fade], axis=1)
        sum_b[h, rows, :] = part
        top_b[h, rows, :] = wide

    upper, lower, every = pl.ds(0, QB), pl.ds(QB, QB), pl.ds(0, TOK)
    @pl.loop(0, HEADS, unroll=2)
    def _(h):
        attend(h, upper, 2, 0, QB, True)
        attend(h, lower, 2, 0, TOK, True)

    @pl.when(me_p >= 1)
    def _():
        ahead(1).wait_recv()
        ahead_z(1).wait_recv()
        finish(1, kvp[1].astype(F32), zp[1].reshape(TOK, HEAD))

        @pl.loop(0, HEADS, unroll=2)
        def _(h):
            attend(h, every, 1, 0, TOK, False)

    @pl.when(me_p >= 2)
    def _():
        ahead(2).wait_recv()
        ahead_z(2).wait_recv()
        finish(0, kvp[0].astype(F32), zp[0].reshape(TOK, HEAD))

        @pl.loop(0, HEADS, unroll=2)
        def _(h):
            attend(h, upper, 0, 0, TOK, False)
            attend(h, lower, 0, QB, QB, False)

    @pl.loop(0, HEADS, unroll=2)
    def _(h):
        both_parts = sum_b[h]
        out[0, :, pl.ds(pl.multiple_of(h * HEAD, HEAD), HEAD)] = (both_parts[:, :HEAD] / both_parts[:, HEAD:]).astype(BF)

    arrived(prv, vpg)

    @pl.loop(0, 2 * OWNERS)
    def _(n):
        store[n, 0] = prv[jnp.clip(list_s[1, n], 0, 31)]

    arrived(r1.at[pl.ds(0, 2 * (OWNERS - 1))], s1)
    arrived(r1.at[pl.ds(0, OWNERS - 1)], s2)
    arrived(zr, srs)
    arrived(zr, sag)
    arrived(prv.at[pl.ds(0, 2 * (OWNERS - 1))], spg)

    @pl.when(me_g < 2)
    def _():
        arrived(r1u.at[pl.ds(0, 2 * 7)], s1u)
        arrived(r1u.at[pl.ds(0, OWNERS - 1)], s2u)

    @pl.when(me_g >= 2)
    def _():
        arrived(r1u.at[pl.ds(0, 2 * 8)], s1u)

    for step in (1, 2):

        @pl.when(me_p < POOL - step)
        def _():
            ahead(step).wait_send()
            ahead_z(step).wait_send()


def rope_table():
    positions = np.arange(2048, dtype=np.float64)[:, None]
    frequency = ROPE_THETA ** (-np.arange(64, dtype=np.float64) * 2.0 / HEAD)
    angle = positions * frequency[None, :]
    return np.concatenate([np.cos(angle), np.sin(angle)], axis=1).astype(np.float32)


def per_device(
    tokens, gain, wq, wk, wv, bq, bk, bv, down, upq, upk, upv, ids, lengths, table
):
    smem = pl.BlockSpec(memory_space=pltpu.SMEM)
    vmem = pl.BlockSpec(memory_space=pltpu.VMEM)
    hbm = pl.BlockSpec(memory_space=pl.ANY)
    V = pltpu.VMEM
    D = pltpu.SemaphoreType.DMA
    scratch = [
        V((8, TOK, CHUNK), BF),
        V((8, CHUNK, 256), BF),
        V((4, WIDTH, 256), BF),
        V((TOK, 256), F32),
        V((TOK, QCOLS), F32),
        V((TOK, HEAD), F32),
        V((TOK, HEAD), F32),
        V((WIDTH,), BF),
        V((QCOLS,), BF),
        V((HEAD,), BF),
        V((HEAD,), BF),
        V((512,), jnp.int32),
        V((74, HEAD), F32),
        V((8, HEAD), jnp.int32),
        pltpu.SMEM((8, HEAD), jnp.int32),
        V((2048, HEAD), F32),
        V((3, TOK, HEAD), F32),
        V((3, TOK, HEAD), F32),
        V((32, 4, 16, 256), BF),
        V((32, 16, HEAD), BF),
        V((4, 4, 16, 256), BF),
        V((4, 16, HEAD), BF),
        V((4, RANK, CHUNK), BF),
        V((2 * RANK, 256), BF),
        V((8, 64, 256), BF),
        V((7, 64, 256), BF),
        V((64, 256), BF),
        V((8, 64, 256), BF),
        V((2, 8, 64, HEAD), BF),
        V((2, 32, PAGE, HEAD), BF),
        V((TOK, 256), BF),
        V((2, TOK, 256), BF),
        V((32, 2, PAGE, HEAD), BF),
        V((32, 2, PAGE, HEAD), BF),
        V((HEADS, TOK, 2 * HEAD), BF),
        V((2 * HEAD, 3 * TOK), BF),
        V((3, TOK, 2 * HEAD), BF),
        V((HEADS, TOK, HEAD), F32),
        V((HEADS, TOK, 2 * HEAD), F32),
        D((8,)), D((8,)), D((4,)), D((7,)),
        D, D, D, D, D, D, D((2,)), D((2,)), D,
        D, D, D, D((2,)), D, D, D((2,)), D((2,)), D,
    ]
    return pl.pallas_call(
        kernel,
        out_shape=(
            jax.ShapeDtypeStruct((1, TOK, QCOLS), BF),
            jax.ShapeDtypeStruct((32, 1, 2, PAGE, HEAD), BF),
        ),
        in_specs=[smem, smem] + [hbm] * 14,
        out_specs=(vmem, vmem),
        scratch_shapes=scratch,
        compiler_params=pltpu.CompilerParams(
            collective_id=0, has_side_effects=True, vmem_limit_bytes=60 * 1024 * 1024
        ),
        name="layer",
    )(ids, lengths, tokens, gain, wq, wk, wv, bq, bk, bv, down, upq, upk, upv, table, jnp.asarray(rope_table()))


def solution(mesh):
    placed = (
        P("group", "pool", None),
        P(),
        P(None, "tensor"),
        P(None, "tensor"),
        P(None, "tensor"),
        P("tensor"),
        P("tensor"),
        P("tensor"),
        P(("pool", "group"), None, None, "tensor"),
        P(("pool", "group"), None, "tensor"),
        P(("pool", "group"), None, "tensor"),
        P(("pool", "group"), None, "tensor"),
        P(),
        P("group", None),
        P(),
    )
    return jax.shard_map(
        per_device,
        mesh=mesh,
        in_specs=placed,
        out_specs=(P("group", "pool", "tensor"), P(("pool", "group"), "tensor", None, None, None)),
        check_vma=False,
    )
```

```python
import functools
import math

import jax
import jax.numpy as jnp
import numpy as np
from jax import lax
from jax.experimental import pallas as pl
from jax.experimental.pallas import tpu as pltpu
from jax.sharding import PartitionSpec as P

HEAD = 128
PAGE = 16
RANK = 64
ADAPTER_SCALE = 2.0
ROPE_THETA = 1000000.0
EPS = 1e-06
MASKED = -1e30
BF = jnp.bfloat16
F32 = jnp.float32
MESH = pl.DeviceIdType.MESH
POOL = 4
GROUP = 4
OWNERS = 16
TENSOR = 8
TOK = 512
WIDTH = 8192
CHUNK = 1024
QCOLS = 1024
HEADS = 8
QB = 256
KWIN = 1280


def dot(a, b):
    return jnp.dot(a, b, preferred_element_type=F32)


def dot_t(a, b):
    return lax.dot_general(a, b, (((1,), (1,)), ((), ())), preferred_element_type=F32)


def kernel(
    ids, lengths, tokens, gain, wq, wk, wv, bq, bk, bv, down, upq, upk, upv, table, rope,
    out, store,
    x, wkv_b, wq_b, acc_kv, acc_q, sq, rsb, gain_b, bq_b, bk_b, bv_b, table_b, vecb, list_v, list_s, rope_b, cosb, sinb,
    r1, r1u, st, stu, fac, upkv, zst, zr, zs, zf, zp,
    kvo, kvb, kvp, pst, prv, qx, kx, vx, top_b, sum_b,
    tok_sem, wkv_sem, wq_sem, misc,
    s1, s1u, s2, s2u, srs, sag, skv, szp, spg,
    v1, v1u, v2, v2u, vrs, vag, vkv, vzp, vpg,
):
    me_p = lax.axis_index("pool")
    me_g = lax.axis_index("group")
    me_t = lax.axis_index("tensor")
    owner = me_p * GROUP + me_g

    def chunk(c):
        return pl.ds(pl.multiple_of(c * CHUNK, CHUNK), CHUNK)

    def tok_copy(c):
        return pltpu.make_async_copy(tokens.at[0, :, chunk(c)], x.at[c], tok_sem.at[c])

    def wkv_start(c):
        for n, src in enumerate((wk, wv)):
            pltpu.make_async_copy(src.at[chunk(c), :], wkv_b.at[c, :, pl.ds(n * HEAD, HEAD)], wkv_sem.at[c]).start()

    def arrived(ref, sem):
        pltpu.make_async_copy(ref, ref, sem).wait()

    def wq_copy(j):
        return pltpu.make_async_copy(wq.at[:, pl.ds(j * 256, 256)], wq_b.at[j], wq_sem.at[j])

    small = [
        pltpu.make_async_copy(src, dst, misc.at[2 + n])
        for n, (src, dst) in enumerate(((gain, gain_b), (bq, bq_b), (bk, bk_b), (bv, bv_b), (table, table_b)))
    ]
    rope_copy = pltpu.make_async_copy(rope, rope_b, misc.at[1])

    upkv[...] = jnp.zeros_like(upkv)

    barrier = pltpu.get_barrier_semaphore()

    def plane(i):
        dest = lax.rem(owner + i, OWNERS)
        return dest // GROUP, lax.rem(dest, GROUP)

    def around(i):
        return lax.rem(me_t + i, TENSOR)

    @pl.loop(1, OWNERS)
    def _(i):
        dp, dg = plane(i)
        pl.semaphore_signal(barrier, inc=1, device_id=(dp, dg, me_t), device_id_type=MESH)

    @pl.loop(1, TENSOR)
    def _(i):
        pl.semaphore_signal(barrier, inc=1, device_id=(me_p, me_g, around(i)), device_id_type=MESH)

    for cp in small:
        cp.start()
    for c in range(2):
        tok_copy(c).start()
        wkv_start(c)

    pl.semaphore_wait(barrier, OWNERS - 1 + TENSOR - 1)

    mine2 = pl.ds(owner * 2, 2)

    def rows_of(dp):
        return pl.ds(pl.multiple_of(dp * 16, 16), 16)

    def cols_of(dg):
        return pl.ds(pl.multiple_of(dg * 256, 256), 256)

    def remote(src, dst, send, recv, dp, dg, dt):
        return pltpu.make_async_remote_copy(
            src_ref=src, dst_ref=dst, send_sem=send, recv_sem=recv,
            device_id=(dp, dg, dt), device_id_type=MESH,
        )

    for n, src in enumerate((upk, upv)):
        for dp in range(POOL):
            dest = dp * GROUP + n

            @pl.when(dest != owner)
            def _():
                remote(src.at[:, pl.ds(dp * 16, 16), :], r1u.at[mine2], s1u, v1u, dp, n, me_t).start()

        @pl.when(me_g == n)
        def _():
            pltpu.make_async_copy(src.at[:, rows_of(me_p), :], r1u.at[mine2], v1u).start()

    @pl.loop(1, OWNERS)
    def _(i):
        dp, dg = plane(i)
        rows, cols = rows_of(dp), cols_of(dg)
        remote(down.at[:, :, rows, cols], r1.at[mine2, pl.ds(0, 3)], s1, v1, dp, dg, me_t).start()
        remote(upq.at[:, rows, cols], r1.at[mine2, 3], s1, v1, dp, dg, me_t).start()

    pltpu.make_async_copy(down.at[:, :, rows_of(me_p), cols_of(me_g)], r1.at[mine2, pl.ds(0, 3)], v1).start()
    pltpu.make_async_copy(upq.at[:, rows_of(me_p), cols_of(me_g)], r1.at[mine2, 3], v1).start()

    for c in range(2, 8):
        tok_copy(c).start()
        wkv_start(c)
    rope_copy.start()
    for j in range(4):
        wq_copy(j).start()

    sq[...] = jnp.zeros_like(sq)
    acc_kv[...] = jnp.zeros_like(acc_kv)
    for cp in small:
        cp.wait()
    for c in range(8):
        vecb[pl.ds(c * 8, 8), :] = gain_b[pl.ds(c * CHUNK, CHUNK)].astype(F32).reshape(8, HEAD)
    vecb[pl.ds(64, 8), :] = bq_b[...].astype(F32).reshape(8, HEAD)
    vecb[pl.ds(72, 1), :] = bk_b[...].astype(F32).reshape(1, HEAD)
    vecb[pl.ds(73, 1), :] = bv_b[...].astype(F32).reshape(1, HEAD)

    @pl.loop(0, 8)
    def _(c):
        tok_copy(c).wait()

        @pl.loop(0, TOK // 64)
        def _(r):
            rows = pl.ds(pl.multiple_of(r * 64, 64), 64)
            s = sq[rows, :]
            for k in range(CHUNK // 128):
                lanes = pl.ds(k * 128, 128)
                part = x[c, rows, lanes].astype(F32)
                s = s + part * part
                x[c, rows, lanes] = (part * vecb[pl.ds(c * 8 + k, 1), :]).astype(BF)
            sq[rows, :] = s

        arrived(wkv_b.at[c], wkv_sem.at[c])
        acc_kv[...] += dot(x[c], wkv_b[c])

    mean = jnp.sum(sq[...], axis=1, keepdims=True) * (1.0 / WIDTH)
    rsb[...] = jnp.broadcast_to(lax.rsqrt(mean + EPS), (TOK, HEAD))

    def bias(n):
        return vecb[pl.ds(64 + n, 1), :]

    def q_tile(j):
        wq_copy(j).wait()
        cols = pl.ds(j * 256, 256)
        acc_q[:, cols] = dot(x[0], wq_b[j, pl.ds(0, CHUNK), :])

        @pl.loop(1, 8)
        def _(c):
            acc_q[:, cols] += dot(x[c], wq_b[j, chunk(c), :])

    kv_base = acc_kv[...] * jnp.concatenate([rsb[...], rsb[...]], axis=1)
    kv_base = kv_base + jnp.concatenate([bias(8), bias(9)], axis=1)
    acc_kv[...] = kv_base
    kvb[...] = kv_base.astype(BF)

    def make_lists():
        shape = (32, HEAD)
        list_v[...] = jnp.zeros_like(list_v)
        sub = lax.broadcasted_iota(jnp.int32, shape, 0)
        lan = lax.broadcasted_iota(jnp.int32, shape, 1)
        slots = table_b[...].reshape(4, HEAD)
        wide = [jnp.broadcast_to(slots[r : r + 1, :], shape) for r in range(4)]
        mine = jnp.where(me_g < 2, jnp.where(me_g == 0, wide[0], wide[1]), jnp.where(me_g == 2, wide[2], wide[3]))
        first = me_p * 32

        def column(v, where):
            return jnp.sum(jnp.where(where, v, 0), axis=1, keepdims=True)

        def row(v, where):
            return jnp.sum(jnp.where(where, v, 0), axis=0, keepdims=True)

        own = column(mine, lan == sub + first)
        inside = (lan >= first) & (lan < first + 32)
        order = column(1, inside & (mine < own))
        list_v[pl.ds(0, 1), :] = row(sub, order == lan)
        source = jnp.zeros((32, 1), jnp.int32)
        for r in range(4):
            source = source + column(lan // 32 * GROUP + r, wide[r] == sub + owner * 32)
        as_row = row(jnp.broadcast_to(source, shape), lan == sub)
        item = source * 2 + column(1, (as_row == source) & (lan < sub))
        list_v[pl.ds(1, 1), :] = row(jnp.broadcast_to(item, shape), lan == sub)
        pltpu.make_async_copy(list_v, list_s, misc.at[0]).start()

    q_tile(0)
    q_tile(1)

    arrived(r1, v1)
    for g in range(GROUP):
        st[g, pl.ds(0, 2)] = r1[ids[g], pl.ds(1, 2)]
        st[g, 2] = r1[ids[g], 0]
        st[g, 3] = r1[ids[g], 3]

    @pl.loop(1, OWNERS)
    def _(i):
        dp, dg = plane(i)
        remote(st.at[dg], fac.at[:, rows_of(me_p), cols_of(me_g)], s2, v2, dp, dg, me_t).start()

    pltpu.make_async_copy(st.at[me_g], fac.at[:, rows_of(me_p), cols_of(me_g)], v2).start()

    def up_place(n):
        first = RANK * n + me_p * 16
        return upkv.at[pl.ds(pl.multiple_of(first, 16), 16), pl.ds(n * HEAD, HEAD)]

    for n in range(2):

        @pl.when(me_g == n)
        def _():
            arrived(r1u, v1u)
            for g in range(GROUP):
                stu[g] = r1u[ids[g]]

            @pl.loop(1, OWNERS)
            def _(i):
                dp, dg = plane(i)
                remote(stu.at[dg], up_place(n), s2u, v2u.at[n], dp, dg, me_t).start()

            pltpu.make_async_copy(stu.at[me_g], up_place(n), v2u.at[n]).start()

    q_tile(2)
    make_lists()

    arrived(fac, v2)

    def ahead(step):
        return remote(kvb, kvp.at[2 - step], skv.at[step - 1], vkv.at[step - 1], me_p + step, me_g, me_t)

    def ahead_z(step):
        return remote(
            zf.at[:, :, pl.ds(0, HEAD)], zp.at[2 - step], szp.at[step - 1], vzp.at[step - 1], me_p + step, me_g, me_t
        )

    for step in (1, 2):

        @pl.when(me_p < POOL - step)
        def _():
            ahead(step).start()

    z = dot_t(x[me_t], fac[...].reshape(4 * RANK, CHUNK))
    zst[...] = z.astype(BF).reshape(TENSOR, TOK // TENSOR, 4 * RANK)

    @pl.loop(1, TENSOR)
    def _(i):
        dt = around(i)
        remote(zst.at[dt], zr.at[i - 1], srs, vrs, me_p, me_g, dt).start()

    q_tile(3)
    arrived(zr, vrs)
    total = zst[me_t].astype(F32)
    for i in range(TENSOR - 1):
        total = total + zr[i].astype(F32)
    mine = rsb[pl.ds(pl.multiple_of(me_t * 64, 64), 64), :] * ADAPTER_SCALE
    zs[...] = (total * jnp.concatenate([mine, mine], axis=1)).astype(BF)

    @pl.loop(1, TENSOR)
    def _(i):
        remote(zs, zf.at[me_t], sag, vag, me_p, me_g, around(i)).start()

    pltpu.make_async_copy(zs, zf.at[me_t], vag).start()
    rope_copy.wait()
    start1 = lengths[0, 0]
    start2 = lengths[0, 0] + lengths[0, 1]
    lane = lax.broadcasted_iota(jnp.int32, (TOK, HEAD), 1)
    low = lane < HEAD // 2

    def both(row, low_mask):
        turned = pltpu.roll(row, HEAD // 2, 1)
        return jnp.where(low_mask, row, turned), jnp.where(low_mask, turned, row)

    low8 = lax.broadcasted_iota(jnp.int32, (8, HEAD), 1) < HEAD // 2

    def start_row(at):
        return both(jnp.broadcast_to(rope_b[pl.ds(at, 1), :], (8, HEAD)), low8)

    c1, n1 = start_row(start1)
    c2, n2 = start_row(start2)

    def rotation(n):
        first = (me_p + (n - 2)) * TOK
        token = first + lax.broadcasted_iota(jnp.int32, (TOK, HEAD), 0)
        tc, tn = both(rope_b[pl.ds(pl.multiple_of(first, TOK), TOK), :], low)
        in1 = token >= start1
        in2 = token >= start2
        sc = jnp.where(in2, c2[0:1, :], jnp.where(in1, c1[0:1, :], 1.0))
        sn = jnp.where(in2, n2[0:1, :], jnp.where(in1, n1[0:1, :], 0.0))
        cosb[n] = tc * sc + tn * sn
        swung = tn * sc - tc * sn
        sinb[n] = jnp.where(low, -swung, swung)
        return in1.astype(jnp.int32) + in2.astype(jnp.int32)

    segment = rotation(2)
    marks = jnp.where((lane < 4) & (lane != segment), MASKED, 0.0).astype(BF)
    for h in range(HEADS):
        qx[h, :, pl.ds(HEAD, HEAD)] = marks
    mark_row = lax.broadcasted_iota(jnp.int32, (HEAD, 3 * TOK), 0)
    ktok = (me_p - 2) * TOK + lax.broadcasted_iota(jnp.int32, (HEAD, 3 * TOK), 1)
    kseg = (ktok >= start1).astype(jnp.int32) + (ktok >= start2).astype(jnp.int32)
    kx[pl.ds(HEAD, HEAD), :] = (mark_row == kseg).astype(F32).astype(BF)
    vx[:, pl.ds(HEAD, HEAD)] = jnp.ones((3 * TOK, HEAD), BF)
    for n in range(2):

        @pl.when(me_p + n >= 2)
        def _():
            rotation(n)

    for n in range(2):
        arrived(upkv.at[pl.ds(RANK * n, RANK), pl.ds(n * HEAD, HEAD)], v2u.at[n])
    arrived(zf, vag)
    for step in (1, 2):

        @pl.when(me_p < POOL - step)
        def _():
            ahead_z(step).start()

    def rotated(v, n):
        return v * cosb[n] + pltpu.roll(v, HEAD // 2, 1) * sinb[n]

    def finish(n, base, z):
        kv = base + dot(z, upkv[...])
        key = rotated(kv[:, :HEAD], n).astype(BF)
        value = kv[:, HEAD:].astype(BF)
        kx[pl.ds(0, HEAD), pl.ds(n * TOK, TOK)] = key.T
        vx[pl.ds(n * TOK, TOK), pl.ds(0, HEAD)] = value
        return key, value

    key, value = finish(2, acc_kv[...], zf[:, :, pl.ds(0, HEAD)].reshape(TOK, HEAD))
    kvo[0] = key.reshape(TOK // PAGE, PAGE, HEAD)
    kvo[1] = value.reshape(TOK // PAGE, PAGE, HEAD)

    pltpu.make_async_copy(list_v, list_s, misc.at[0]).wait()

    @pl.loop(0, 2 * OWNERS)
    def _(n):
        page = jnp.clip(list_s[0, n], 0, 31)
        pst[n, 0] = kvo[0, page]
        pst[n, 1] = kvo[1, page]

    @pl.loop(1, OWNERS)
    def _(i):
        dp, dg = plane(i)
        dest = dp * GROUP + dg
        remote(pst.at[pl.ds(dest * 2, 2)], prv.at[mine2], spg, vpg, dp, dg, me_t).start()

    pltpu.make_async_copy(pst.at[mine2], prv.at[mine2], vpg).start()

    for j in range(4):
        low_rank = dot(zf[:, :, pl.ds(HEAD, HEAD)].reshape(TOK, HEAD)[:, :RANK], fac[3, :, pl.ds(j * 256, 256)])
        for h in range(2):
            head = acc_q[:, pl.ds(j * 256 + h * HEAD, HEAD)] * rsb[...] + bias(2 * j + h)
            head = head + low_rank[:, h * HEAD : (h + 1) * HEAD]
            qx[2 * j + h, :, pl.ds(0, HEAD)] = (rotated(head, 2) * (HEAD**-0.5 * math.log2(math.e))).astype(BF)

    pair_rows = lax.rem(lax.broadcasted_iota(jnp.int32, (2 * QB, QB), 0), QB)
    causal = pair_rows >= lax.broadcasted_iota(jnp.int32, (2 * QB, QB), 1)

    def heads_of(step):
        return pl.ds(2 * step[0], 2), pl.ds(step[1] * QB, QB)

    def scores(step):
        heads, rows = heads_of(step)
        return dot(qx[heads, rows, :].reshape(2 * QB, 2 * HEAD), kx[:, pl.ds(step[2], step[3])])

    def put(step, ratio):
        heads, rows = heads_of(step)
        for n in range(2):
            out[0, rows, pl.ds((2 * step[0] + n) * HEAD, HEAD)] = ratio[n * QB : (n + 1) * QB].astype(BF)

    def own_step(step, score):
        heads, rows = heads_of(step)
        count = step[3]
        last = jnp.where(causal, score[:, count - QB :], MASKED)
        score = last if count == QB else jnp.concatenate([score[:, : count - QB], last], axis=1)
        top = jnp.max(score, axis=1, keepdims=True)
        weight = jnp.exp2(score - top).astype(BF)
        part = dot(weight, vx[pl.ds(step[2], count), :])
        sum_b[heads, rows, :] = part.reshape(2, QB, 2 * HEAD)
        top_b[heads, rows, :] = jnp.broadcast_to(top, (2 * QB, HEAD)).reshape(2, QB, HEAD)

    def earlier_step(step, score):
        heads, rows = heads_of(step)
        before = top_b[heads, rows, :].reshape(2 * QB, HEAD)
        top = jnp.maximum(before[:, :1], jnp.max(score, axis=1, keepdims=True))
        weight = jnp.exp2(score - top).astype(BF)
        part = dot(weight, vx[pl.ds(step[2], step[3]), :])
        fade = jnp.exp2(before - top)
        old = sum_b[heads, rows, :].reshape(2 * QB, 2 * HEAD)
        put(step, (part[:, :HEAD] + old[:, :HEAD] * fade) / (part[:, HEAD:] + old[:, HEAD:] * fade))

    def run(steps, act):
        score = scores(steps[0])
        for n, step in enumerate(steps):
            following = scores(steps[n + 1]) if n + 1 < len(steps) else None
            act(step, score)
            score = following

    pairs = range(HEADS // 2)
    run([(h, b, 2 * TOK, (b + 1) * QB) for h in pairs for b in range(2)], own_step)

    @pl.when(me_p == 0)
    def _():
        for h in pairs:
            for b in range(2):
                heads, rows = heads_of((h, b))
                old = sum_b[heads, rows, :].reshape(2 * QB, 2 * HEAD)
                put((h, b), old[:, :HEAD] / old[:, HEAD:])

    def take(step):
        ahead(step).wait_recv()
        ahead_z(step).wait_recv()
        n = 2 - step
        finish(n, kvp[n].astype(F32), zp[n].reshape(TOK, HEAD))

    @pl.when(me_p == 1)
    def _():
        take(1)
        run([(h, b, TOK, TOK) for h in pairs for b in range(2)], earlier_step)

    @pl.when(me_p >= 2)
    def _():
        take(1)
        take(2)
        run([(h, b, b * QB, 2 * TOK - b * QB) for h in pairs for b in range(2)], earlier_step)

    arrived(prv, vpg)

    @pl.loop(0, 2 * OWNERS)
    def _(n):
        store[n, 0] = prv[jnp.clip(list_s[1, n], 0, 31)]

    arrived(r1.at[pl.ds(0, 2 * (OWNERS - 1))], s1)
    arrived(r1.at[pl.ds(0, OWNERS - 1)], s2)
    arrived(zr, srs)
    arrived(zr, sag)
    arrived(prv.at[pl.ds(0, 2 * (OWNERS - 1))], spg)

    @pl.when(me_g < 2)
    def _():
        arrived(r1u.at[pl.ds(0, 2 * 7)], s1u)
        arrived(r1u.at[pl.ds(0, OWNERS - 1)], s2u)

    @pl.when(me_g >= 2)
    def _():
        arrived(r1u.at[pl.ds(0, 2 * 8)], s1u)

    for step in (1, 2):

        @pl.when(me_p < POOL - step)
        def _():
            ahead(step).wait_send()
            ahead_z(step).wait_send()


def hand_over(out, store, out_to, store_to, out_b, store_b, come, go):
    parts = [(out.at[0, pl.ds(n * 128, 128)], out_b.at[pl.ds(n * 128, 128)], out_to.at[0, pl.ds(n * 128, 128)]) for n in range(4)]
    parts.append((store, store_b, store_to))
    for n, (src, held, _) in enumerate(parts):
        pltpu.make_async_copy(src, held, come.at[n]).start()
    for n, (src, held, dst) in enumerate(parts):
        pltpu.make_async_copy(src, held, come.at[n]).wait()
        pltpu.make_async_copy(held, dst, go.at[n]).start()
    for n, (_, held, dst) in enumerate(parts):
        pltpu.make_async_copy(held, dst, go.at[n]).wait()


def rope_table():
    positions = np.arange(2048, dtype=np.float64)[:, None]
    frequency = ROPE_THETA ** (-np.arange(64, dtype=np.float64) * 2.0 / HEAD)
    angle = positions * frequency[None, :]
    return np.concatenate([np.cos(angle), np.sin(angle)], axis=1).astype(np.float32)


def per_device(
    tokens, gain, wq, wk, wv, bq, bk, bv, down, upq, upk, upv, ids, lengths, table
):
    smem = pl.BlockSpec(memory_space=pltpu.SMEM)
    vmem = pl.BlockSpec(memory_space=pltpu.VMEM)
    hbm = pl.BlockSpec(memory_space=pl.ANY)
    V = pltpu.VMEM
    D = pltpu.SemaphoreType.DMA
    scratch = [
        V((8, TOK, CHUNK), BF),
        V((8, CHUNK, 256), BF),
        V((4, WIDTH, 256), BF),
        V((TOK, 256), F32),
        V((TOK, QCOLS), F32),
        V((TOK, HEAD), F32),
        V((TOK, HEAD), F32),
        V((WIDTH,), BF),
        V((QCOLS,), BF),
        V((HEAD,), BF),
        V((HEAD,), BF),
        V((512,), jnp.int32),
        V((74, HEAD), F32),
        V((8, HEAD), jnp.int32),
        pltpu.SMEM((8, HEAD), jnp.int32),
        V((2048, HEAD), F32),
        V((3, TOK, HEAD), F32),
        V((3, TOK, HEAD), F32),
        V((32, 4, 16, 256), BF),
        V((32, 16, HEAD), BF),
        V((4, 4, 16, 256), BF),
        V((4, 16, HEAD), BF),
        V((4, RANK, CHUNK), BF),
        V((2 * RANK, 256), BF),
        V((8, 64, 256), BF),
        V((7, 64, 256), BF),
        V((64, 256), BF),
        V((8, 64, 256), BF),
        V((2, 8, 64, HEAD), BF),
        V((2, 32, PAGE, HEAD), BF),
        V((TOK, 256), BF),
        V((2, TOK, 256), BF),
        V((32, 2, PAGE, HEAD), BF),
        V((32, 2, PAGE, HEAD), BF),
        V((HEADS, TOK, 2 * HEAD), BF),
        V((2 * HEAD, 3 * TOK), BF),
        V((3 * TOK, 2 * HEAD), BF),
        V((HEADS, TOK, HEAD), F32),
        V((HEADS, TOK, 2 * HEAD), F32),
        D((8,)), D((8,)), D((4,)), D((7,)),
        D, D, D, D, D, D, D((2,)), D((2,)), D,
        D, D, D, D((2,)), D, D, D((2,)), D((2,)), D,
    ]
    made = pl.pallas_call(
        kernel,
        out_shape=(
            jax.ShapeDtypeStruct((1, TOK, QCOLS), BF),
            jax.ShapeDtypeStruct((32, 1, 2, PAGE, HEAD), BF),
        ),
        in_specs=[smem, smem] + [hbm] * 14,
        out_specs=(vmem, vmem),
        scratch_shapes=scratch,
        compiler_params=pltpu.CompilerParams(
            collective_id=0, has_side_effects=True, vmem_limit_bytes=60 * 1024 * 1024
        ),
        name="layer",
    )(ids, lengths, tokens, gain, wq, wk, wv, bq, bk, bv, down, upq, upk, upv, table, jnp.asarray(rope_table()))
    return pl.pallas_call(
        hand_over,
        out_shape=tuple(jax.ShapeDtypeStruct(m.shape, m.dtype) for m in made),
        in_specs=[hbm, hbm],
        out_specs=(hbm, hbm),
        scratch_shapes=[V((TOK, QCOLS), BF), V((32, 1, 2, PAGE, HEAD), BF), D((5,)), D((5,))],
        name="hand_over",
    )(*made)


def solution(mesh):
    placed = (
        P("group", "pool", None),
        P(),
        P(None, "tensor"),
        P(None, "tensor"),
        P(None, "tensor"),
        P("tensor"),
        P("tensor"),
        P("tensor"),
        P(("pool", "group"), None, None, "tensor"),
        P(("pool", "group"), None, "tensor"),
        P(("pool", "group"), None, "tensor"),
        P(("pool", "group"), None, "tensor"),
        P(),
        P("group", None),
        P(),
    )
    return jax.shard_map(
        per_device,
        mesh=mesh,
        in_specs=placed,
        out_specs=(P("group", "pool", "tensor"), P(("pool", "group"), "tensor", None, None, None)),
        check_vma=False,
    )
```

```python
import functools
import math

import jax
import jax.numpy as jnp
import numpy as np
from jax import lax
from jax.experimental import pallas as pl
from jax.experimental.pallas import tpu as pltpu
from jax.sharding import PartitionSpec as P

HEAD = 128
PAGE = 16
RANK = 64
ADAPTER_SCALE = 2.0
ROPE_THETA = 1000000.0
EPS = 1e-06
MASKED = -1e30
BF = jnp.bfloat16
F32 = jnp.float32
MESH = pl.DeviceIdType.MESH
POOL = 4
GROUP = 4
OWNERS = 16
TENSOR = 8
TOK = 512
WIDTH = 8192
CHUNK = 1024
QCOLS = 1024
HEADS = 8
QB = 256
KWIN = 1280


def dot(a, b):
    return jnp.dot(a, b, preferred_element_type=F32)


def dot_t(a, b):
    return lax.dot_general(a, b, (((1,), (1,)), ((), ())), preferred_element_type=F32)


def kernel(
    single,
    ids, lengths, tokens, gain, wq, wk, wv, bq, bk, bv, down, upq, upk, upv, table, rope,
    out, store,
    x, wkv_b, wq_b, acc_kv, acc_q, sq, rsb, gain_b, bq_b, bk_b, bv_b, table_b, vecb, list_v, list_s, rope_b, cosb, sinb,
    bank_b, bank_u, pick_b, pick_u, r1, r1u, st, stu, fac, upkv, zst, zr, zs, zf, zp,
    kvo, kvb, kvp, pst, prv, qx, kx, vx, top_b, sum_b,
    tok_sem, wkv_sem, wq_sem, misc, bank_sem,
    s1, s1u, s2, s2u, srs, sag, skv, szp, spg,
    v1, v1u, v2, v2u, vrs, vag, vkv, vzp, vpg,
):
    me_p = lax.axis_index("pool")
    me_g = lax.axis_index("group")
    me_t = lax.axis_index("tensor")
    owner = me_p * GROUP + me_g

    def chunk(c):
        return pl.ds(pl.multiple_of(c * CHUNK, CHUNK), CHUNK)

    def tok_copy(c):
        return pltpu.make_async_copy(tokens.at[0, :, chunk(c)], x.at[c], tok_sem.at[c])

    def wkv_start(c):
        for n, src in enumerate((wk, wv)):
            pltpu.make_async_copy(src.at[chunk(c), :], wkv_b.at[c, :, pl.ds(n * HEAD, HEAD)], wkv_sem.at[c]).start()

    def arrived(ref, sem):
        pltpu.make_async_copy(ref, ref, sem).wait()

    def wq_copy(j):
        return pltpu.make_async_copy(wq.at[:, pl.ds(j * 256, 256)], wq_b.at[j], wq_sem.at[j])

    small = [
        pltpu.make_async_copy(src, dst, misc.at[2 + n])
        for n, (src, dst) in enumerate(((gain, gain_b), (bq, bq_b), (bk, bk_b), (bv, bv_b), (table, table_b)))
    ]
    rope_copy = pltpu.make_async_copy(rope, rope_b, misc.at[1])

    upkv[...] = jnp.zeros_like(upkv)

    barrier = pltpu.get_barrier_semaphore()

    def plane(i):
        dest = lax.rem(owner + i, OWNERS)
        return dest // GROUP, lax.rem(dest, GROUP)

    def around(i):
        return lax.rem(me_t + i, TENSOR)

    @pl.loop(1, OWNERS)
    def _(i):
        dp, dg = plane(i)
        pl.semaphore_signal(barrier, inc=1, device_id=(dp, dg, me_t), device_id_type=MESH)

    @pl.loop(1, TENSOR)
    def _(i):
        pl.semaphore_signal(barrier, inc=1, device_id=(me_p, me_g, around(i)), device_id_type=MESH)

    if single:
        pltpu.make_async_copy(down, bank_b.at[:, pl.ds(0, 3)], bank_sem.at[0]).start()
        pltpu.make_async_copy(upq, bank_b.at[:, 3], bank_sem.at[0]).start()
        for n, src in enumerate((upk, upv)):
            pltpu.make_async_copy(src, bank_u.at[n], bank_sem.at[1]).start()
    for cp in small:
        cp.start()
    for c in range(2):
        tok_copy(c).start()
        wkv_start(c)

    per_owner = 1 if single else 2

    def entry(g):
        return lax.div(ids[g], 2) if single else ids[g]

    if single:
        slot = jnp.int32(0)
        for g in range(GROUP):
            slot = jnp.where(lax.div(ids[g], 2) == owner, lax.rem(ids[g], 2), slot)
        arrived(bank_b, bank_sem.at[0])
        arrived(bank_u, bank_sem.at[1])
        pick_b[...] = bank_b[slot]
        for n in range(2):
            pick_u[n] = bank_u[n, slot]

    pl.semaphore_wait(barrier, OWNERS - 1 + TENSOR - 1)

    mine2 = pl.ds(owner * 2, 2)

    def rows_of(dp):
        return pl.ds(pl.multiple_of(dp * 16, 16), 16)

    def cols_of(dg):
        return pl.ds(pl.multiple_of(dg * 256, 256), 256)

    def remote(src, dst, send, recv, dp, dg, dt):
        return pltpu.make_async_remote_copy(
            src_ref=src, dst_ref=dst, send_sem=send, recv_sem=recv,
            device_id=(dp, dg, dt), device_id_type=MESH,
        )

    def main_parts(rows, cols):
        if single:
            return ((pick_b.at[:, rows, cols], r1.at[owner]),)
        return (
            (down.at[:, :, rows, cols], r1.at[mine2, pl.ds(0, 3)]),
            (upq.at[:, rows, cols], r1.at[mine2, 3]),
        )

    def up_part(n, rows):
        if single:
            return pick_u.at[n, rows], r1u.at[owner]
        return (upk, upv)[n].at[:, rows, :], r1u.at[mine2]

    for n in range(2):
        for dp in range(POOL):
            dest = dp * GROUP + n

            @pl.when(dest != owner)
            def _():
                src, dst = up_part(n, pl.ds(dp * 16, 16))
                remote(src, dst, s1u, v1u, dp, n, me_t).start()

        @pl.when(me_g == n)
        def _():
            src, dst = up_part(n, rows_of(me_p))
            pltpu.make_async_copy(src, dst, v1u).start()

    @pl.loop(1, OWNERS)
    def _(i):
        dp, dg = plane(i)
        for src, dst in main_parts(rows_of(dp), cols_of(dg)):
            remote(src, dst, s1, v1, dp, dg, me_t).start()

    for src, dst in main_parts(rows_of(me_p), cols_of(me_g)):
        pltpu.make_async_copy(src, dst, v1).start()

    for c in range(2, 8):
        tok_copy(c).start()
        wkv_start(c)
    rope_copy.start()
    for j in range(4):
        wq_copy(j).start()

    sq[...] = jnp.zeros_like(sq)
    acc_kv[...] = jnp.zeros_like(acc_kv)
    for cp in small:
        cp.wait()
    for c in range(8):
        vecb[pl.ds(c * 8, 8), :] = gain_b[pl.ds(c * CHUNK, CHUNK)].astype(F32).reshape(8, HEAD)
    vecb[pl.ds(64, 8), :] = bq_b[...].astype(F32).reshape(8, HEAD)
    vecb[pl.ds(72, 1), :] = bk_b[...].astype(F32).reshape(1, HEAD)
    vecb[pl.ds(73, 1), :] = bv_b[...].astype(F32).reshape(1, HEAD)

    @pl.loop(0, 8)
    def _(c):
        tok_copy(c).wait()

        @pl.loop(0, TOK // 64)
        def _(r):
            rows = pl.ds(pl.multiple_of(r * 64, 64), 64)
            s = sq[rows, :]
            for k in range(CHUNK // 128):
                lanes = pl.ds(k * 128, 128)
                part = x[c, rows, lanes].astype(F32)
                s = s + part * part
                x[c, rows, lanes] = (part * vecb[pl.ds(c * 8 + k, 1), :]).astype(BF)
            sq[rows, :] = s

        arrived(wkv_b.at[c], wkv_sem.at[c])
        acc_kv[...] += dot(x[c], wkv_b[c])

    mean = jnp.sum(sq[...], axis=1, keepdims=True) * (1.0 / WIDTH)
    rsb[...] = jnp.broadcast_to(lax.rsqrt(mean + EPS), (TOK, HEAD))

    def bias(n):
        return vecb[pl.ds(64 + n, 1), :]

    def q_tile(j):
        wq_copy(j).wait()
        cols = pl.ds(j * 256, 256)
        acc_q[:, cols] = dot(x[0], wq_b[j, pl.ds(0, CHUNK), :])

        @pl.loop(1, 8)
        def _(c):
            acc_q[:, cols] += dot(x[c], wq_b[j, chunk(c), :])

    kv_base = acc_kv[...] * jnp.concatenate([rsb[...], rsb[...]], axis=1)
    kv_base = kv_base + jnp.concatenate([bias(8), bias(9)], axis=1)
    acc_kv[...] = kv_base
    kvb[...] = kv_base.astype(BF)

    def make_lists():
        shape = (32, HEAD)
        list_v[...] = jnp.zeros_like(list_v)
        sub = lax.broadcasted_iota(jnp.int32, shape, 0)
        lan = lax.broadcasted_iota(jnp.int32, shape, 1)
        slots = table_b[...].reshape(4, HEAD)
        wide = [jnp.broadcast_to(slots[r : r + 1, :], shape) for r in range(4)]
        mine = jnp.where(me_g < 2, jnp.where(me_g == 0, wide[0], wide[1]), jnp.where(me_g == 2, wide[2], wide[3]))
        first = me_p * 32

        def column(v, where):
            return jnp.sum(jnp.where(where, v, 0), axis=1, keepdims=True)

        def row(v, where):
            return jnp.sum(jnp.where(where, v, 0), axis=0, keepdims=True)

        own = column(mine, lan == sub + first)
        inside = (lan >= first) & (lan < first + 32)
        order = column(1, inside & (mine < own))
        list_v[pl.ds(0, 1), :] = row(sub, order == lan)
        source = jnp.zeros((32, 1), jnp.int32)
        for r in range(4):
            source = source + column(lan // 32 * GROUP + r, wide[r] == sub + owner * 32)
        as_row = row(jnp.broadcast_to(source, shape), lan == sub)
        item = source * 2 + column(1, (as_row == source) & (lan < sub))
        list_v[pl.ds(1, 1), :] = row(jnp.broadcast_to(item, shape), lan == sub)
        pltpu.make_async_copy(list_v, list_s, misc.at[0]).start()

    if not single:
        q_tile(0)
        q_tile(1)

    arrived(r1.at[pl.ds(0, per_owner * OWNERS)], v1)
    for g in range(GROUP):
        st[g, pl.ds(0, 2)] = r1[entry(g), pl.ds(1, 2)]
        st[g, 2] = r1[entry(g), 0]
        st[g, 3] = r1[entry(g), 3]

    @pl.loop(1, OWNERS)
    def _(i):
        dp, dg = plane(i)
        remote(st.at[dg], fac.at[:, rows_of(me_p), cols_of(me_g)], s2, v2, dp, dg, me_t).start()

    pltpu.make_async_copy(st.at[me_g], fac.at[:, rows_of(me_p), cols_of(me_g)], v2).start()

    def up_place(n):
        first = RANK * n + me_p * 16
        return upkv.at[pl.ds(pl.multiple_of(first, 16), 16), pl.ds(n * HEAD, HEAD)]

    for n in range(2):

        @pl.when(me_g == n)
        def _():
            arrived(r1u.at[pl.ds(0, per_owner * OWNERS)], v1u)
            for g in range(GROUP):
                stu[g] = r1u[entry(g)]

            @pl.loop(1, OWNERS)
            def _(i):
                dp, dg = plane(i)
                remote(stu.at[dg], up_place(n), s2u, v2u.at[n], dp, dg, me_t).start()

            pltpu.make_async_copy(stu.at[me_g], up_place(n), v2u.at[n]).start()

    if single:
        q_tile(0)
        q_tile(1)
    q_tile(2)
    make_lists()

    arrived(fac, v2)

    def ahead(step):
        return remote(kvb, kvp.at[2 - step], skv.at[step - 1], vkv.at[step - 1], me_p + step, me_g, me_t)

    def ahead_z(step):
        return remote(
            zf.at[:, :, pl.ds(0, HEAD)], zp.at[2 - step], szp.at[step - 1], vzp.at[step - 1], me_p + step, me_g, me_t
        )

    for step in (1, 2):

        @pl.when(me_p < POOL - step)
        def _():
            ahead(step).start()

    z = dot_t(x[me_t], fac[...].reshape(4 * RANK, CHUNK))
    zst[...] = z.astype(BF).reshape(TENSOR, TOK // TENSOR, 4 * RANK)

    @pl.loop(1, TENSOR)
    def _(i):
        dt = around(i)
        remote(zst.at[dt], zr.at[i - 1], srs, vrs, me_p, me_g, dt).start()

    q_tile(3)
    arrived(zr, vrs)
    total = zst[me_t].astype(F32)
    for i in range(TENSOR - 1):
        total = total + zr[i].astype(F32)
    mine = rsb[pl.ds(pl.multiple_of(me_t * 64, 64), 64), :] * ADAPTER_SCALE
    zs[...] = (total * jnp.concatenate([mine, mine], axis=1)).astype(BF)

    @pl.loop(1, TENSOR)
    def _(i):
        remote(zs, zf.at[me_t], sag, vag, me_p, me_g, around(i)).start()

    pltpu.make_async_copy(zs, zf.at[me_t], vag).start()
    rope_copy.wait()
    start1 = lengths[0, 0]
    start2 = lengths[0, 0] + lengths[0, 1]
    lane = lax.broadcasted_iota(jnp.int32, (TOK, HEAD), 1)
    low = lane < HEAD // 2

    def both(row, low_mask):
        turned = pltpu.roll(row, HEAD // 2, 1)
        return jnp.where(low_mask, row, turned), jnp.where(low_mask, turned, row)

    low8 = lax.broadcasted_iota(jnp.int32, (8, HEAD), 1) < HEAD // 2

    def start_row(at):
        return both(jnp.broadcast_to(rope_b[pl.ds(at, 1), :], (8, HEAD)), low8)

    c1, n1 = start_row(start1)
    c2, n2 = start_row(start2)

    def rotation(n):
        first = (me_p + (n - 2)) * TOK
        token = first + lax.broadcasted_iota(jnp.int32, (TOK, HEAD), 0)
        tc, tn = both(rope_b[pl.ds(pl.multiple_of(first, TOK), TOK), :], low)
        in1 = token >= start1
        in2 = token >= start2
        sc = jnp.where(in2, c2[0:1, :], jnp.where(in1, c1[0:1, :], 1.0))
        sn = jnp.where(in2, n2[0:1, :], jnp.where(in1, n1[0:1, :], 0.0))
        cosb[n] = tc * sc + tn * sn
        swung = tn * sc - tc * sn
        sinb[n] = jnp.where(low, -swung, swung)
        return in1.astype(jnp.int32) + in2.astype(jnp.int32)

    segment = rotation(2)
    marks = jnp.where((lane < 4) & (lane != segment), MASKED, 0.0).astype(BF)
    for h in range(HEADS):
        qx[h, :, pl.ds(HEAD, HEAD)] = marks
    mark_row = lax.broadcasted_iota(jnp.int32, (HEAD, 3 * TOK), 0)
    ktok = (me_p - 2) * TOK + lax.broadcasted_iota(jnp.int32, (HEAD, 3 * TOK), 1)
    kseg = (ktok >= start1).astype(jnp.int32) + (ktok >= start2).astype(jnp.int32)
    kx[pl.ds(HEAD, HEAD), :] = (mark_row == kseg).astype(F32).astype(BF)
    vx[:, pl.ds(HEAD, HEAD)] = jnp.ones((3 * TOK, HEAD), BF)
    for n in range(2):

        @pl.when(me_p + n >= 2)
        def _():
            rotation(n)

    for n in range(2):
        arrived(upkv.at[pl.ds(RANK * n, RANK), pl.ds(n * HEAD, HEAD)], v2u.at[n])
    arrived(zf, vag)
    for step in (1, 2):

        @pl.when(me_p < POOL - step)
        def _():
            ahead_z(step).start()

    def rotated(v, n):
        return v * cosb[n] + pltpu.roll(v, HEAD // 2, 1) * sinb[n]

    def finish(n, base, z):
        kv = base + dot(z, upkv[...])
        key = rotated(kv[:, :HEAD], n).astype(BF)
        value = kv[:, HEAD:].astype(BF)
        kx[pl.ds(0, HEAD), pl.ds(n * TOK, TOK)] = key.T
        vx[pl.ds(n * TOK, TOK), pl.ds(0, HEAD)] = value
        return key, value

    key, value = finish(2, acc_kv[...], zf[:, :, pl.ds(0, HEAD)].reshape(TOK, HEAD))
    kvo[0] = key.reshape(TOK // PAGE, PAGE, HEAD)
    kvo[1] = value.reshape(TOK // PAGE, PAGE, HEAD)

    pltpu.make_async_copy(list_v, list_s, misc.at[0]).wait()

    @pl.loop(0, 2 * OWNERS)
    def _(n):
        page = jnp.clip(list_s[0, n], 0, 31)
        pst[n, 0] = kvo[0, page]
        pst[n, 1] = kvo[1, page]

    @pl.loop(1, OWNERS)
    def _(i):
        dp, dg = plane(i)
        dest = dp * GROUP + dg
        remote(pst.at[pl.ds(dest * 2, 2)], prv.at[mine2], spg, vpg, dp, dg, me_t).start()

    pltpu.make_async_copy(pst.at[mine2], prv.at[mine2], vpg).start()

    for j in range(4):
        low_rank = dot(zf[:, :, pl.ds(HEAD, HEAD)].reshape(TOK, HEAD)[:, :RANK], fac[3, :, pl.ds(j * 256, 256)])
        for h in range(2):
            head = acc_q[:, pl.ds(j * 256 + h * HEAD, HEAD)] * rsb[...] + bias(2 * j + h)
            head = head + low_rank[:, h * HEAD : (h + 1) * HEAD]
            qx[2 * j + h, :, pl.ds(0, HEAD)] = (rotated(head, 2) * (HEAD**-0.5 * math.log2(math.e))).astype(BF)

    pair_rows = lax.rem(lax.broadcasted_iota(jnp.int32, (2 * QB, QB), 0), QB)
    causal = pair_rows >= lax.broadcasted_iota(jnp.int32, (2 * QB, QB), 1)

    def heads_of(step):
        return pl.ds(2 * step[0], 2), pl.ds(step[1] * QB, QB)

    def scores(step):
        heads, rows = heads_of(step)
        return dot(qx[heads, rows, :].reshape(2 * QB, 2 * HEAD), kx[:, pl.ds(step[2], step[3])])

    def put(step, ratio):
        heads, rows = heads_of(step)
        for n in range(2):
            out[0, rows, pl.ds((2 * step[0] + n) * HEAD, HEAD)] = ratio[n * QB : (n + 1) * QB].astype(BF)

    def own_step(step, score):
        heads, rows = heads_of(step)
        count = step[3]
        last = jnp.where(causal, score[:, count - QB :], MASKED)
        score = last if count == QB else jnp.concatenate([score[:, : count - QB], last], axis=1)
        top = jnp.max(score, axis=1, keepdims=True)
        weight = jnp.exp2(score - top).astype(BF)
        part = dot(weight, vx[pl.ds(step[2], count), :])
        sum_b[heads, rows, :] = part.reshape(2, QB, 2 * HEAD)
        top_b[heads, rows, :] = jnp.broadcast_to(top, (2 * QB, HEAD)).reshape(2, QB, HEAD)

    def earlier_step(step, score):
        heads, rows = heads_of(step)
        before = top_b[heads, rows, :].reshape(2 * QB, HEAD)
        top = jnp.maximum(before[:, :1], jnp.max(score, axis=1, keepdims=True))
        weight = jnp.exp2(score - top).astype(BF)
        part = dot(weight, vx[pl.ds(step[2], step[3]), :])
        fade = jnp.exp2(before - top)
        old = sum_b[heads, rows, :].reshape(2 * QB, 2 * HEAD)
        put(step, (part[:, :HEAD] + old[:, :HEAD] * fade) / (part[:, HEAD:] + old[:, HEAD:] * fade))

    def run(steps, act):
        score = scores(steps[0])
        for n, step in enumerate(steps):
            following = scores(steps[n + 1]) if n + 1 < len(steps) else None
            act(step, score)
            score = following

    pairs = range(HEADS // 2)
    run([(h, b, 2 * TOK, (b + 1) * QB) for h in pairs for b in range(2)], own_step)

    @pl.when(me_p == 0)
    def _():
        for h in pairs:
            for b in range(2):
                heads, rows = heads_of((h, b))
                old = sum_b[heads, rows, :].reshape(2 * QB, 2 * HEAD)
                put((h, b), old[:, :HEAD] / old[:, HEAD:])

    def take(step):
        ahead(step).wait_recv()
        ahead_z(step).wait_recv()
        n = 2 - step
        finish(n, kvp[n].astype(F32), zp[n].reshape(TOK, HEAD))

    @pl.when(me_p == 1)
    def _():
        take(1)
        run([(h, b, TOK, TOK) for h in pairs for b in range(2)], earlier_step)

    @pl.when(me_p >= 2)
    def _():
        take(1)
        take(2)
        run([(h, b, b * QB, 2 * TOK - b * QB) for h in pairs for b in range(2)], earlier_step)

    arrived(prv, vpg)

    @pl.loop(0, 2 * OWNERS)
    def _(n):
        store[n, 0] = prv[jnp.clip(list_s[1, n], 0, 31)]

    arrived(r1.at[pl.ds(0, per_owner * (OWNERS - 1))], s1)
    arrived(r1.at[pl.ds(0, OWNERS - 1)], s2)
    arrived(zr, srs)
    arrived(zr, sag)
    arrived(prv.at[pl.ds(0, 2 * (OWNERS - 1))], spg)

    @pl.when(me_g < 2)
    def _():
        arrived(r1u.at[pl.ds(0, per_owner * 7)], s1u)
        arrived(r1u.at[pl.ds(0, OWNERS - 1)], s2u)

    @pl.when(me_g >= 2)
    def _():
        arrived(r1u.at[pl.ds(0, per_owner * 8)], s1u)

    for step in (1, 2):

        @pl.when(me_p < POOL - step)
        def _():
            ahead(step).wait_send()
            ahead_z(step).wait_send()


def hand_over(out, store, out_to, store_to, out_b, store_b, come, go):
    parts = [(out.at[0, pl.ds(n * 128, 128)], out_b.at[pl.ds(n * 128, 128)], out_to.at[0, pl.ds(n * 128, 128)]) for n in range(4)]
    parts.append((store, store_b, store_to))
    for n, (src, held, _) in enumerate(parts):
        pltpu.make_async_copy(src, held, come.at[n]).start()
    for n, (src, held, dst) in enumerate(parts):
        pltpu.make_async_copy(src, held, come.at[n]).wait()
        pltpu.make_async_copy(held, dst, go.at[n]).start()
    for n, (_, held, dst) in enumerate(parts):
        pltpu.make_async_copy(held, dst, go.at[n]).wait()


def rope_table():
    positions = np.arange(2048, dtype=np.float64)[:, None]
    frequency = ROPE_THETA ** (-np.arange(64, dtype=np.float64) * 2.0 / HEAD)
    angle = positions * frequency[None, :]
    return np.concatenate([np.cos(angle), np.sin(angle)], axis=1).astype(np.float32)


def per_device(
    tokens, gain, wq, wk, wv, bq, bk, bv, down, upq, upk, upv, ids, lengths, table
):
    smem = pl.BlockSpec(memory_space=pltpu.SMEM)
    vmem = pl.BlockSpec(memory_space=pltpu.VMEM)
    hbm = pl.BlockSpec(memory_space=pl.ANY)
    V = pltpu.VMEM
    D = pltpu.SemaphoreType.DMA
    scratch = [
        V((8, TOK, CHUNK), BF),
        V((8, CHUNK, 256), BF),
        V((4, WIDTH, 256), BF),
        V((TOK, 256), F32),
        V((TOK, QCOLS), F32),
        V((TOK, HEAD), F32),
        V((TOK, HEAD), F32),
        V((WIDTH,), BF),
        V((QCOLS,), BF),
        V((HEAD,), BF),
        V((HEAD,), BF),
        V((512,), jnp.int32),
        V((74, HEAD), F32),
        V((8, HEAD), jnp.int32),
        pltpu.SMEM((8, HEAD), jnp.int32),
        V((2048, HEAD), F32),
        V((3, TOK, HEAD), F32),
        V((3, TOK, HEAD), F32),
        V((2, 4, RANK, CHUNK), BF),
        V((2, 2, RANK, HEAD), BF),
        V((4, RANK, CHUNK), BF),
        V((2, RANK, HEAD), BF),
        V((32, 4, 16, 256), BF),
        V((32, 16, HEAD), BF),
        V((4, 4, 16, 256), BF),
        V((4, 16, HEAD), BF),
        V((4, RANK, CHUNK), BF),
        V((2 * RANK, 256), BF),
        V((8, 64, 256), BF),
        V((7, 64, 256), BF),
        V((64, 256), BF),
        V((8, 64, 256), BF),
        V((2, 8, 64, HEAD), BF),
        V((2, 32, PAGE, HEAD), BF),
        V((TOK, 256), BF),
        V((2, TOK, 256), BF),
        V((32, 2, PAGE, HEAD), BF),
        V((32, 2, PAGE, HEAD), BF),
        V((HEADS, TOK, 2 * HEAD), BF),
        V((2 * HEAD, 3 * TOK), BF),
        V((3 * TOK, 2 * HEAD), BF),
        V((HEADS, TOK, HEAD), F32),
        V((HEADS, TOK, 2 * HEAD), F32),
        D((8,)), D((8,)), D((4,)), D((7,)), D((2,)),
        D, D, D, D, D, D, D((2,)), D((2,)), D,
        D, D, D, D((2,)), D, D, D((2,)), D((2,)), D,
    ]
    def layer(single):
        return pl.pallas_call(
            functools.partial(kernel, single),
            out_shape=(
                jax.ShapeDtypeStruct((1, TOK, QCOLS), BF),
                jax.ShapeDtypeStruct((32, 1, 2, PAGE, HEAD), BF),
            ),
            in_specs=[smem, smem] + [hbm] * 14,
            out_specs=(vmem, vmem),
            scratch_shapes=scratch,
            compiler_params=pltpu.CompilerParams(
                collective_id=1 if single else 0, has_side_effects=True, vmem_limit_bytes=60 * 1024 * 1024
            ),
            name="layer_single" if single else "layer",
        )

    both = jnp.any((ids[:, None] ^ ids[None, :]) == 1)
    operands = (ids, lengths, tokens, gain, wq, wk, wv, bq, bk, bv, down, upq, upk, upv, table, jnp.asarray(rope_table()))
    made = lax.cond(both, layer(False), layer(True), *operands)
    return pl.pallas_call(
        hand_over,
        out_shape=tuple(jax.ShapeDtypeStruct(m.shape, m.dtype) for m in made),
        in_specs=[hbm, hbm],
        out_specs=(hbm, hbm),
        scratch_shapes=[V((TOK, QCOLS), BF), V((32, 1, 2, PAGE, HEAD), BF), D((5,)), D((5,))],
        name="hand_over",
    )(*made)


def solution(mesh):
    placed = (
        P("group", "pool", None),
        P(),
        P(None, "tensor"),
        P(None, "tensor"),
        P(None, "tensor"),
        P("tensor"),
        P("tensor"),
        P("tensor"),
        P(("pool", "group"), None, None, "tensor"),
        P(("pool", "group"), None, "tensor"),
        P(("pool", "group"), None, "tensor"),
        P(("pool", "group"), None, "tensor"),
        P(),
        P("group", None),
        P(),
    )
    return jax.shard_map(
        per_device,
        mesh=mesh,
        in_specs=placed,
        out_specs=(P("group", "pool", "tensor"), P(("pool", "group"), "tensor", None, None, None)),
        check_vma=False,
    )
```

```python
import functools
import math

import jax
import jax.numpy as jnp
import numpy as np
from jax import lax
from jax.experimental import pallas as pl
from jax.experimental.pallas import tpu as pltpu
from jax.sharding import PartitionSpec as P

HEAD = 128
PAGE = 16
RANK = 64
ADAPTER_SCALE = 2.0
ROPE_THETA = 1000000.0
EPS = 1e-06
MASKED = -1e30
BF = jnp.bfloat16
F32 = jnp.float32
MESH = pl.DeviceIdType.MESH
POOL = 4
GROUP = 4
OWNERS = 16
TENSOR = 8
TOK = 512
WIDTH = 8192
CHUNK = 1024
QCOLS = 1024
HEADS = 8
QB = 256
KWIN = 1280


def dot(a, b):
    return jnp.dot(a, b, preferred_element_type=F32)


def dot_t(a, b):
    return lax.dot_general(a, b, (((1,), (1,)), ((), ())), preferred_element_type=F32)


def kernel(
    single,
    ids, lengths, tokens, gain, wq, wk, wv, bq, bk, bv, down, upq, upk, upv, table, rope,
    out, store,
    x, wkv_b, wq_b, acc_kv, acc_q, sq, rsb, gain_b, bq_b, bk_b, bv_b, table_b, vecb, list_v, list_s, rope_b, cosb, sinb,
    bank_b, bank_u, pick_b, pick_u, r1, r1u, st, stu, fac, upkv, zst, zr, zs, zf, zp,
    kvo, kvb, kvp, pst, prv, qx, kx, vx, top_b, sum_b,
    tok_sem, wkv_sem, wq_sem, misc, bank_sem,
    s1, s1u, s2, s2u, srs, sag, skv, szp, spg,
    v1, v1u, v2, v2u, vrs, vag, vkv, vzp, vpg,
):
    me_p = lax.axis_index("pool")
    me_g = lax.axis_index("group")
    me_t = lax.axis_index("tensor")
    owner = me_p * GROUP + me_g

    def chunk(c):
        return pl.ds(pl.multiple_of(c * CHUNK, CHUNK), CHUNK)

    def tok_copy(c):
        return pltpu.make_async_copy(tokens.at[0, :, chunk(c)], x.at[c], tok_sem.at[c])

    def wkv_start(c):
        for n, src in enumerate((wk, wv)):
            pltpu.make_async_copy(src.at[chunk(c), :], wkv_b.at[c, :, pl.ds(n * HEAD, HEAD)], wkv_sem.at[c]).start()

    def arrived(ref, sem):
        pltpu.make_async_copy(ref, ref, sem).wait()

    def wq_copy(j):
        return pltpu.make_async_copy(wq.at[:, pl.ds(j * 256, 256)], wq_b.at[j], wq_sem.at[j])

    small = [
        pltpu.make_async_copy(src, dst, misc.at[2 + n])
        for n, (src, dst) in enumerate(((gain, gain_b), (bq, bq_b), (bk, bk_b), (bv, bv_b), (table, table_b)))
    ]
    rope_copy = pltpu.make_async_copy(rope, rope_b, misc.at[1])

    if single:
        pltpu.make_async_copy(down, bank_b.at[:, pl.ds(0, 3)], bank_sem.at[0]).start()
        pltpu.make_async_copy(upq, bank_b.at[:, 3], bank_sem.at[0]).start()
        for n, src in enumerate((upk, upv)):
            pltpu.make_async_copy(src, bank_u.at[n], bank_sem.at[1]).start()

    upkv[...] = jnp.zeros_like(upkv)

    barrier = pltpu.get_barrier_semaphore()

    def plane(i):
        dest = lax.rem(owner + i, OWNERS)
        return dest // GROUP, lax.rem(dest, GROUP)

    def around(i):
        return lax.rem(me_t + i, TENSOR)

    @pl.loop(1, OWNERS)
    def _(i):
        dp, dg = plane(i)
        pl.semaphore_signal(barrier, inc=1, device_id=(dp, dg, me_t), device_id_type=MESH)

    @pl.loop(1, TENSOR)
    def _(i):
        pl.semaphore_signal(barrier, inc=1, device_id=(me_p, me_g, around(i)), device_id_type=MESH)

    for cp in small:
        cp.start()
    for c in range(2):
        tok_copy(c).start()
        wkv_start(c)

    per_owner = 1 if single else 2

    def entry(g):
        return lax.div(ids[g], 2) if single else ids[g]

    if single:
        slot = jnp.int32(0)
        for g in range(GROUP):
            slot = jnp.where(lax.div(ids[g], 2) == owner, lax.rem(ids[g], 2), slot)
        arrived(bank_b, bank_sem.at[0])
        arrived(bank_u, bank_sem.at[1])
        pick_b[...] = bank_b[slot]
        for n in range(2):
            pick_u[n] = bank_u[n, slot]

    for c in range(2, 8):
        tok_copy(c).start()
        wkv_start(c)
    rope_copy.start()
    for j in range(4):
        wq_copy(j).start()

    pl.semaphore_wait(barrier, OWNERS - 1 + TENSOR - 1)

    mine2 = pl.ds(owner * 2, 2)

    def rows_of(dp):
        return pl.ds(pl.multiple_of(dp * 16, 16), 16)

    def cols_of(dg):
        return pl.ds(pl.multiple_of(dg * 256, 256), 256)

    def remote(src, dst, send, recv, dp, dg, dt):
        return pltpu.make_async_remote_copy(
            src_ref=src, dst_ref=dst, send_sem=send, recv_sem=recv,
            device_id=(dp, dg, dt), device_id_type=MESH,
        )

    def main_parts(rows, cols):
        if single:
            return ((pick_b.at[:, rows, cols], r1.at[owner]),)
        return (
            (down.at[:, :, rows, cols], r1.at[mine2, pl.ds(0, 3)]),
            (upq.at[:, rows, cols], r1.at[mine2, 3]),
        )

    def up_part(n, rows):
        if single:
            return pick_u.at[n, rows], r1u.at[owner]
        return (upk, upv)[n].at[:, rows, :], r1u.at[mine2]

    for n in range(2):
        for dp in range(POOL):
            dest = dp * GROUP + n

            @pl.when(dest != owner)
            def _():
                src, dst = up_part(n, pl.ds(dp * 16, 16))
                remote(src, dst, s1u, v1u, dp, n, me_t).start()

        @pl.when(me_g == n)
        def _():
            src, dst = up_part(n, rows_of(me_p))
            pltpu.make_async_copy(src, dst, v1u).start()

    @pl.loop(1, OWNERS)
    def _(i):
        dp, dg = plane(i)
        for src, dst in main_parts(rows_of(dp), cols_of(dg)):
            remote(src, dst, s1, v1, dp, dg, me_t).start()

    for src, dst in main_parts(rows_of(me_p), cols_of(me_g)):
        pltpu.make_async_copy(src, dst, v1).start()


    sq[...] = jnp.zeros_like(sq)
    acc_kv[...] = jnp.zeros_like(acc_kv)
    for cp in small:
        cp.wait()
    for c in range(8):
        vecb[pl.ds(c * 8, 8), :] = gain_b[pl.ds(c * CHUNK, CHUNK)].astype(F32).reshape(8, HEAD)
    vecb[pl.ds(64, 8), :] = bq_b[...].astype(F32).reshape(8, HEAD)
    vecb[pl.ds(72, 1), :] = bk_b[...].astype(F32).reshape(1, HEAD)
    vecb[pl.ds(73, 1), :] = bv_b[...].astype(F32).reshape(1, HEAD)

    @pl.loop(0, 8)
    def _(c):
        tok_copy(c).wait()

        @pl.loop(0, TOK // 64)
        def _(r):
            rows = pl.ds(pl.multiple_of(r * 64, 64), 64)
            s = sq[rows, :]
            for k in range(CHUNK // 128):
                lanes = pl.ds(k * 128, 128)
                part = x[c, rows, lanes].astype(F32)
                s = s + part * part
                x[c, rows, lanes] = (part * vecb[pl.ds(c * 8 + k, 1), :]).astype(BF)
            sq[rows, :] = s

        arrived(wkv_b.at[c], wkv_sem.at[c])
        acc_kv[...] += dot(x[c], wkv_b[c])

    mean = jnp.sum(sq[...], axis=1, keepdims=True) * (1.0 / WIDTH)
    rsb[...] = jnp.broadcast_to(lax.rsqrt(mean + EPS), (TOK, HEAD))

    def bias(n):
        return vecb[pl.ds(64 + n, 1), :]

    def q_tile(j):
        wq_copy(j).wait()
        cols = pl.ds(j * 256, 256)
        acc_q[:, cols] = dot(x[0], wq_b[j, pl.ds(0, CHUNK), :])

        @pl.loop(1, 8)
        def _(c):
            acc_q[:, cols] += dot(x[c], wq_b[j, chunk(c), :])

    kv_base = acc_kv[...] * jnp.concatenate([rsb[...], rsb[...]], axis=1)
    kv_base = kv_base + jnp.concatenate([bias(8), bias(9)], axis=1)
    acc_kv[...] = kv_base
    kvb[...] = kv_base.astype(BF)

    def make_lists():
        shape = (32, HEAD)
        list_v[...] = jnp.zeros_like(list_v)
        sub = lax.broadcasted_iota(jnp.int32, shape, 0)
        lan = lax.broadcasted_iota(jnp.int32, shape, 1)
        slots = table_b[...].reshape(4, HEAD)
        wide = [jnp.broadcast_to(slots[r : r + 1, :], shape) for r in range(4)]
        mine = jnp.where(me_g < 2, jnp.where(me_g == 0, wide[0], wide[1]), jnp.where(me_g == 2, wide[2], wide[3]))
        first = me_p * 32

        def column(v, where):
            return jnp.sum(jnp.where(where, v, 0), axis=1, keepdims=True)

        def row(v, where):
            return jnp.sum(jnp.where(where, v, 0), axis=0, keepdims=True)

        own = column(mine, lan == sub + first)
        inside = (lan >= first) & (lan < first + 32)
        order = column(1, inside & (mine < own))
        list_v[pl.ds(0, 1), :] = row(sub, order == lan)
        source = jnp.zeros((32, 1), jnp.int32)
        for r in range(4):
            source = source + column(lan // 32 * GROUP + r, wide[r] == sub + owner * 32)
        as_row = row(jnp.broadcast_to(source, shape), lan == sub)
        item = source * 2 + column(1, (as_row == source) & (lan < sub))
        list_v[pl.ds(1, 1), :] = row(jnp.broadcast_to(item, shape), lan == sub)
        pltpu.make_async_copy(list_v, list_s, misc.at[0]).start()

    if not single:
        q_tile(0)
        q_tile(1)

    arrived(r1.at[pl.ds(0, per_owner * OWNERS)], v1)
    for g in range(GROUP):
        st[g, pl.ds(0, 2)] = r1[entry(g), pl.ds(1, 2)]
        st[g, 2] = r1[entry(g), 0]
        st[g, 3] = r1[entry(g), 3]

    @pl.loop(1, OWNERS)
    def _(i):
        dp, dg = plane(i)
        remote(st.at[dg], fac.at[:, rows_of(me_p), cols_of(me_g)], s2, v2, dp, dg, me_t).start()

    pltpu.make_async_copy(st.at[me_g], fac.at[:, rows_of(me_p), cols_of(me_g)], v2).start()

    def up_place(n):
        first = RANK * n + me_p * 16
        return upkv.at[pl.ds(pl.multiple_of(first, 16), 16), pl.ds(n * HEAD, HEAD)]

    for n in range(2):

        @pl.when(me_g == n)
        def _():
            arrived(r1u.at[pl.ds(0, per_owner * OWNERS)], v1u)
            for g in range(GROUP):
                stu[g] = r1u[entry(g)]

            @pl.loop(1, OWNERS)
            def _(i):
                dp, dg = plane(i)
                remote(stu.at[dg], up_place(n), s2u, v2u.at[n], dp, dg, me_t).start()

            pltpu.make_async_copy(stu.at[me_g], up_place(n), v2u.at[n]).start()

    if single:
        q_tile(0)
        q_tile(1)
    q_tile(2)
    make_lists()

    arrived(fac, v2)

    def ahead(step):
        return remote(kvb, kvp.at[2 - step], skv.at[step - 1], vkv.at[step - 1], me_p + step, me_g, me_t)

    def ahead_z(step):
        return remote(
            zf.at[:, :, pl.ds(0, HEAD)], zp.at[2 - step], szp.at[step - 1], vzp.at[step - 1], me_p + step, me_g, me_t
        )

    for step in (1, 2):

        @pl.when(me_p < POOL - step)
        def _():
            ahead(step).start()

    z = dot_t(x[me_t], fac[...].reshape(4 * RANK, CHUNK))
    zst[...] = z.astype(BF).reshape(TENSOR, TOK // TENSOR, 4 * RANK)

    @pl.loop(1, TENSOR)
    def _(i):
        dt = around(i)
        remote(zst.at[dt], zr.at[i - 1], srs, vrs, me_p, me_g, dt).start()

    rope_copy.wait()
    start1 = lengths[0, 0]
    start2 = lengths[0, 0] + lengths[0, 1]
    lane = lax.broadcasted_iota(jnp.int32, (TOK, HEAD), 1)
    low = lane < HEAD // 2

    def both(row, low_mask):
        turned = pltpu.roll(row, HEAD // 2, 1)
        return jnp.where(low_mask, row, turned), jnp.where(low_mask, turned, row)

    low8 = lax.broadcasted_iota(jnp.int32, (8, HEAD), 1) < HEAD // 2

    def start_row(at):
        return both(jnp.broadcast_to(rope_b[pl.ds(at, 1), :], (8, HEAD)), low8)

    c1, n1 = start_row(start1)
    c2, n2 = start_row(start2)

    def rotation(n):
        first = (me_p + (n - 2)) * TOK
        token = first + lax.broadcasted_iota(jnp.int32, (TOK, HEAD), 0)
        tc, tn = both(rope_b[pl.ds(pl.multiple_of(first, TOK), TOK), :], low)
        in1 = token >= start1
        in2 = token >= start2
        sc = jnp.where(in2, c2[0:1, :], jnp.where(in1, c1[0:1, :], 1.0))
        sn = jnp.where(in2, n2[0:1, :], jnp.where(in1, n1[0:1, :], 0.0))
        cosb[n] = tc * sc + tn * sn
        swung = tn * sc - tc * sn
        sinb[n] = jnp.where(low, -swung, swung)
        return in1.astype(jnp.int32) + in2.astype(jnp.int32)

    segment = rotation(2)
    marks = jnp.where((lane < 4) & (lane != segment), MASKED, 0.0).astype(BF)
    for h in range(HEADS):
        qx[h, :, pl.ds(HEAD, HEAD)] = marks
    mark_row = lax.broadcasted_iota(jnp.int32, (HEAD, 3 * TOK), 0)
    ktok = (me_p - 2) * TOK + lax.broadcasted_iota(jnp.int32, (HEAD, 3 * TOK), 1)
    kseg = (ktok >= start1).astype(jnp.int32) + (ktok >= start2).astype(jnp.int32)
    kx[pl.ds(HEAD, HEAD), :] = (mark_row == kseg).astype(F32).astype(BF)
    vx[:, pl.ds(HEAD, HEAD)] = jnp.ones((3 * TOK, HEAD), BF)
    for n in range(2):

        @pl.when(me_p + n >= 2)
        def _():
            rotation(n)

    arrived(zr, vrs)
    total = zst[me_t].astype(F32)
    for i in range(TENSOR - 1):
        total = total + zr[i].astype(F32)
    mine = rsb[pl.ds(pl.multiple_of(me_t * 64, 64), 64), :] * ADAPTER_SCALE
    zs[...] = (total * jnp.concatenate([mine, mine], axis=1)).astype(BF)

    @pl.loop(1, TENSOR)
    def _(i):
        remote(zs, zf.at[me_t], sag, vag, me_p, me_g, around(i)).start()

    pltpu.make_async_copy(zs, zf.at[me_t], vag).start()
    q_tile(3)
    for n in range(2):
        arrived(upkv.at[pl.ds(RANK * n, RANK), pl.ds(n * HEAD, HEAD)], v2u.at[n])
    arrived(zf, vag)
    for step in (1, 2):

        @pl.when(me_p < POOL - step)
        def _():
            ahead_z(step).start()

    def rotated(v, n):
        return v * cosb[n] + pltpu.roll(v, HEAD // 2, 1) * sinb[n]

    def finish(n, base, z):
        kv = base + dot(z, upkv[...])
        key = rotated(kv[:, :HEAD], n).astype(BF)
        value = kv[:, HEAD:].astype(BF)
        kx[pl.ds(0, HEAD), pl.ds(n * TOK, TOK)] = key.T
        vx[pl.ds(n * TOK, TOK), pl.ds(0, HEAD)] = value
        return key, value

    key, value = finish(2, acc_kv[...], zf[:, :, pl.ds(0, HEAD)].reshape(TOK, HEAD))
    kvo[0] = key.reshape(TOK // PAGE, PAGE, HEAD)
    kvo[1] = value.reshape(TOK // PAGE, PAGE, HEAD)

    pltpu.make_async_copy(list_v, list_s, misc.at[0]).wait()

    @pl.loop(0, 2 * OWNERS)
    def _(n):
        page = jnp.clip(list_s[0, n], 0, 31)
        pst[n, 0] = kvo[0, page]
        pst[n, 1] = kvo[1, page]

    @pl.loop(1, OWNERS)
    def _(i):
        dp, dg = plane(i)
        dest = dp * GROUP + dg
        remote(pst.at[pl.ds(dest * 2, 2)], prv.at[mine2], spg, vpg, dp, dg, me_t).start()

    pltpu.make_async_copy(pst.at[mine2], prv.at[mine2], vpg).start()

    for j in range(4):
        low_rank = dot(zf[:, :, pl.ds(HEAD, HEAD)].reshape(TOK, HEAD)[:, :RANK], fac[3, :, pl.ds(j * 256, 256)])
        for h in range(2):
            head = acc_q[:, pl.ds(j * 256 + h * HEAD, HEAD)] * rsb[...] + bias(2 * j + h)
            head = head + low_rank[:, h * HEAD : (h + 1) * HEAD]
            qx[2 * j + h, :, pl.ds(0, HEAD)] = (rotated(head, 2) * (HEAD**-0.5 * math.log2(math.e))).astype(BF)

    pair_rows = lax.rem(lax.broadcasted_iota(jnp.int32, (2 * QB, QB), 0), QB)
    causal = pair_rows >= lax.broadcasted_iota(jnp.int32, (2 * QB, QB), 1)

    def heads_of(step):
        return pl.ds(2 * step[0], 2), pl.ds(step[1] * QB, QB)

    def scores(step):
        heads, rows = heads_of(step)
        return dot(qx[heads, rows, :].reshape(2 * QB, 2 * HEAD), kx[:, pl.ds(step[2], step[3])])

    def put(step, ratio):
        heads, rows = heads_of(step)
        for n in range(2):
            out[0, rows, pl.ds((2 * step[0] + n) * HEAD, HEAD)] = ratio[n * QB : (n + 1) * QB].astype(BF)

    def own_step(step, score):
        heads, rows = heads_of(step)
        count = step[3]
        last = jnp.where(causal, score[:, count - QB :], MASKED)
        score = last if count == QB else jnp.concatenate([score[:, : count - QB], last], axis=1)
        top = jnp.max(score, axis=1, keepdims=True)
        weight = jnp.exp2(score - top).astype(BF)
        part = dot(weight, vx[pl.ds(step[2], count), :])
        sum_b[heads, rows, :] = part.reshape(2, QB, 2 * HEAD)
        top_b[heads, rows, :] = jnp.broadcast_to(top, (2 * QB, HEAD)).reshape(2, QB, HEAD)

    def earlier_step(step, score):
        heads, rows = heads_of(step)
        before = top_b[heads, rows, :].reshape(2 * QB, HEAD)
        top = jnp.maximum(before[:, :1], jnp.max(score, axis=1, keepdims=True))
        weight = jnp.exp2(score - top).astype(BF)
        part = dot(weight, vx[pl.ds(step[2], step[3]), :])
        fade = jnp.exp2(before - top)
        old = sum_b[heads, rows, :].reshape(2 * QB, 2 * HEAD)
        put(step, (part[:, :HEAD] + old[:, :HEAD] * fade) / (part[:, HEAD:] + old[:, HEAD:] * fade))

    def run(steps, act):
        score = scores(steps[0])
        for n, step in enumerate(steps):
            following = scores(steps[n + 1]) if n + 1 < len(steps) else None
            act(step, score)
            score = following

    pairs = range(HEADS // 2)
    run([(h, b, 2 * TOK, (b + 1) * QB) for h in pairs for b in range(2)], own_step)

    @pl.when(me_p == 0)
    def _():
        for h in pairs:
            for b in range(2):
                heads, rows = heads_of((h, b))
                old = sum_b[heads, rows, :].reshape(2 * QB, 2 * HEAD)
                put((h, b), old[:, :HEAD] / old[:, HEAD:])

    def take(step):
        ahead(step).wait_recv()
        ahead_z(step).wait_recv()
        n = 2 - step
        finish(n, kvp[n].astype(F32), zp[n].reshape(TOK, HEAD))

    @pl.when(me_p == 1)
    def _():
        take(1)
        run([(h, b, TOK, TOK) for h in pairs for b in range(2)], earlier_step)

    @pl.when(me_p >= 2)
    def _():
        take(1)
        take(2)
        run([(h, b, b * QB, 2 * TOK - b * QB) for h in pairs for b in range(2)], earlier_step)

    arrived(prv, vpg)

    @pl.loop(0, 2 * OWNERS)
    def _(n):
        store[n, 0] = prv[jnp.clip(list_s[1, n], 0, 31)]

    arrived(r1.at[pl.ds(0, per_owner * (OWNERS - 1))], s1)
    arrived(r1.at[pl.ds(0, OWNERS - 1)], s2)
    arrived(zr, srs)
    arrived(zr, sag)
    arrived(prv.at[pl.ds(0, 2 * (OWNERS - 1))], spg)

    @pl.when(me_g < 2)
    def _():
        arrived(r1u.at[pl.ds(0, per_owner * 7)], s1u)
        arrived(r1u.at[pl.ds(0, OWNERS - 1)], s2u)

    @pl.when(me_g >= 2)
    def _():
        arrived(r1u.at[pl.ds(0, per_owner * 8)], s1u)

    for step in (1, 2):

        @pl.when(me_p < POOL - step)
        def _():
            ahead(step).wait_send()
            ahead_z(step).wait_send()


def hand_over(out, store, out_to, store_to, out_b, store_b, come, go):
    parts = [(out.at[0, pl.ds(n * 128, 128)], out_b.at[pl.ds(n * 128, 128)], out_to.at[0, pl.ds(n * 128, 128)]) for n in range(4)]
    parts.append((store, store_b, store_to))
    for n, (src, held, _) in enumerate(parts):
        pltpu.make_async_copy(src, held, come.at[n]).start()
    for n, (src, held, dst) in enumerate(parts):
        pltpu.make_async_copy(src, held, come.at[n]).wait()
        pltpu.make_async_copy(held, dst, go.at[n]).start()
    for n, (_, held, dst) in enumerate(parts):
        pltpu.make_async_copy(held, dst, go.at[n]).wait()


def rope_table():
    positions = np.arange(2048, dtype=np.float64)[:, None]
    frequency = ROPE_THETA ** (-np.arange(64, dtype=np.float64) * 2.0 / HEAD)
    angle = positions * frequency[None, :]
    return np.concatenate([np.cos(angle), np.sin(angle)], axis=1).astype(np.float32)


def per_device(
    tokens, gain, wq, wk, wv, bq, bk, bv, down, upq, upk, upv, ids, lengths, table
):
    smem = pl.BlockSpec(memory_space=pltpu.SMEM)
    vmem = pl.BlockSpec(memory_space=pltpu.VMEM)
    hbm = pl.BlockSpec(memory_space=pl.ANY)
    V = pltpu.VMEM
    D = pltpu.SemaphoreType.DMA
    scratch = [
        V((8, TOK, CHUNK), BF),
        V((8, CHUNK, 256), BF),
        V((4, WIDTH, 256), BF),
        V((TOK, 256), F32),
        V((TOK, QCOLS), F32),
        V((TOK, HEAD), F32),
        V((TOK, HEAD), F32),
        V((WIDTH,), BF),
        V((QCOLS,), BF),
        V((HEAD,), BF),
        V((HEAD,), BF),
        V((512,), jnp.int32),
        V((74, HEAD), F32),
        V((8, HEAD), jnp.int32),
        pltpu.SMEM((8, HEAD), jnp.int32),
        V((2048, HEAD), F32),
        V((3, TOK, HEAD), F32),
        V((3, TOK, HEAD), F32),
        V((2, 4, RANK, CHUNK), BF),
        V((2, 2, RANK, HEAD), BF),
        V((4, RANK, CHUNK), BF),
        V((2, RANK, HEAD), BF),
        V((32, 4, 16, 256), BF),
        V((32, 16, HEAD), BF),
        V((4, 4, 16, 256), BF),
        V((4, 16, HEAD), BF),
        V((4, RANK, CHUNK), BF),
        V((2 * RANK, 256), BF),
        V((8, 64, 256), BF),
        V((7, 64, 256), BF),
        V((64, 256), BF),
        V((8, 64, 256), BF),
        V((2, 8, 64, HEAD), BF),
        V((2, 32, PAGE, HEAD), BF),
        V((TOK, 256), BF),
        V((2, TOK, 256), BF),
        V((32, 2, PAGE, HEAD), BF),
        V((32, 2, PAGE, HEAD), BF),
        V((HEADS, TOK, 2 * HEAD), BF),
        V((2 * HEAD, 3 * TOK), BF),
        V((3 * TOK, 2 * HEAD), BF),
        V((HEADS, TOK, HEAD), F32),
        V((HEADS, TOK, 2 * HEAD), F32),
        D((8,)), D((8,)), D((4,)), D((7,)), D((2,)),
        D, D, D, D, D, D, D((2,)), D((2,)), D,
        D, D, D, D((2,)), D, D, D((2,)), D((2,)), D,
    ]
    def layer(single):
        return pl.pallas_call(
            functools.partial(kernel, single),
            out_shape=(
                jax.ShapeDtypeStruct((1, TOK, QCOLS), BF),
                jax.ShapeDtypeStruct((32, 1, 2, PAGE, HEAD), BF),
            ),
            in_specs=[smem, smem] + [hbm] * 14,
            out_specs=(vmem, vmem),
            scratch_shapes=scratch,
            compiler_params=pltpu.CompilerParams(
                collective_id=1 if single else 0, has_side_effects=True, vmem_limit_bytes=60 * 1024 * 1024
            ),
            name="layer_single" if single else "layer",
        )

    both = jnp.any((ids[:, None] ^ ids[None, :]) == 1)
    operands = (ids, lengths, tokens, gain, wq, wk, wv, bq, bk, bv, down, upq, upk, upv, table, jnp.asarray(rope_table()))
    made = lax.cond(both, layer(False), layer(True), *operands)
    return pl.pallas_call(
        hand_over,
        out_shape=tuple(jax.ShapeDtypeStruct(m.shape, m.dtype) for m in made),
        in_specs=[hbm, hbm],
        out_specs=(hbm, hbm),
        scratch_shapes=[V((TOK, QCOLS), BF), V((32, 1, 2, PAGE, HEAD), BF), D((5,)), D((5,))],
        name="hand_over",
    )(*made)


def solution(mesh):
    placed = (
        P("group", "pool", None),
        P(),
        P(None, "tensor"),
        P(None, "tensor"),
        P(None, "tensor"),
        P("tensor"),
        P("tensor"),
        P("tensor"),
        P(("pool", "group"), None, None, "tensor"),
        P(("pool", "group"), None, "tensor"),
        P(("pool", "group"), None, "tensor"),
        P(("pool", "group"), None, "tensor"),
        P(),
        P("group", None),
        P(),
    )
    return jax.shard_map(
        per_device,
        mesh=mesh,
        in_specs=placed,
        out_specs=(P("group", "pool", "tensor"), P(("pool", "group"), "tensor", None, None, None)),
        check_vma=False,
    )
```
